128 devices in a mesh: ctx: 64 (over z, y, x), tp: 2 (over core).
Axes of the slice: x: 4, y: 4, z: 4, core: 2. Of those that a mesh axis runs over, the one named last changes fastest.
Arguments:
- queries: bfloat16 [16384, 8192], P(('ctx', 'tp')), may hold values from -6 to 6
- key_matrix: bfloat16 [16384, 1024], P(('ctx', 'tp')), may hold values from -6 to 6
- value_matrix: bfloat16 [16384, 1024], P(('ctx', 'tp')), may hold values from -6 to 6
- attention_output: bfloat16 [16384, 8192], P(('ctx', 'tp')), may hold values from -6 to 6
- output_gradient: bfloat16 [16384, 8192], P(('ctx', 'tp')), may hold values from -6 to 6
- lengths: int32 [256], replicated, may hold values from 1 to 1792, 16384 in all
Outputs:
- query_grad: bfloat16 [16384, 8192], P(('ctx', 'tp'))
- key_gradient: bfloat16 [16384, 1024], P(('ctx', 'tp'))
- value_gradient: bfloat16 [16384, 1024], P(('ctx', 'tp'))
The draws below stay inside these ranges and needn't reach their ends.
Inputs may be any that keep to these rules, and one draw needn't show every extreme that they name: The lengths sum to 16384; the longest document has exactly 1792 tokens.
All inputs are finite; a program needn't handle non-finite values.
Results may differ from the reference program's by a relative error of at most 0.005.
Values may be sent and summed in bfloat16 or wider, within the bound.
A program may use at most 128 MiB of HBM per device.

```python
import math
import jax
import jax.numpy as jnp
import numpy as np
from jax import lax

QUERY_HEADS = 64
KEY_VALUE_HEADS = 8
HEAD_SIZE = 128
T_DEV = 256
REACH = 7
MOST = 1792
PACKED_TOKENS = 16384
DOCS = 256


def draw_queries(key, part):
    key = jax.random.fold_in(key, 11)
    table_entries = jax.random.truncated_normal(key, -4.0, 4.0, (PACKED_TOKENS, QUERY_HEADS * HEAD_SIZE))
    return table_entries.astype(jnp.bfloat16)


def draw_key_matrix(key, part):
    key = jax.random.fold_in(key, 12)
    table_entries = jax.random.truncated_normal(key, -4.0, 4.0, (PACKED_TOKENS, KEY_VALUE_HEADS * HEAD_SIZE))
    return table_entries.astype(jnp.bfloat16)


def level_of(key, shape, cuts, least, largest):
    def one(dim, shards_of):
        heights = jax.random.uniform(jax.random.fold_in(jax.random.fold_in(key, 6), dim), (shards_of,), jnp.float32, least / len(cuts), largest / len(cuts))
        return jnp.repeat(jnp.exp(heights), shape[dim] // shards_of).reshape((-1,) + (1,) * (len(shape) - dim - 1))

    factor_of = one(*cuts[0])
    for cut in cuts[1:]:
        factor_of = factor_of * one(*cut)
    return factor_of


def profile(number_of, total, bound, slope):
    portions = [(1 << 20) // math.isqrt(grade ** slope) + 1 for grade in range(2, number_of + 1)]
    rest, counts = total - bound - (number_of - 1), [1] * (number_of - 1)
    while rest > 0:
        candidates = [i for i in range(number_of - 1) if counts[i] < bound]
        whole, budget = sum([portions[i] for i in candidates]), rest
        for i in candidates:
            extra = min(bound - counts[i], max(1, budget * portions[i] // whole), rest)
            counts[i] = counts[i] + extra
            rest = rest - extra
    return np.array([bound] + counts)


def uneven(rng, number_of, total, bound, slope):
    if number_of == 2:
        one = jax.random.randint(rng, (), max(1, total - bound), min(bound, total - 1) + 1)
        return jnp.stack([one, total - one])
    sizes = jnp.asarray(profile(number_of, total, bound, slope), jnp.int32)
    couples = (number_of - 1) // 2
    donor, sink = sizes[1:1 + 2 * couples:2], sizes[2:2 + 2 * couples:2]
    margin = jnp.minimum(donor - 1, bound - sink)
    moved = jax.random.randint(jax.random.fold_in(rng, 1), (couples,), 0, 1 << 20) % (margin + 1)
    sizes = sizes.at[1:1 + 2 * couples:2].set(donor - moved).at[2:2 + 2 * couples:2].set(sink + moved)
    return sizes[jax.random.permutation(jax.random.fold_in(rng, 2), number_of)]


def noise(rng, extent, width, most, pieces=(), kind=jnp.bfloat16):
    factor_of = level_of(rng, extent, pieces, -0.22, 0.18) if pieces else 1.0
    drawn = jax.random.normal(rng, extent, jnp.float32) * width * factor_of
    return jnp.minimum(jnp.maximum(drawn, -most), most).astype(kind)


def setup_inputs(seed: int = 0) -> dict:
    key_list = jax.random.split(jax.random.key(seed), 7)
    return {
        "queries": draw_queries(jax.random.fold_in(key_list[6], 71), 0),
        "key_matrix": draw_key_matrix(jax.random.fold_in(key_list[6], 71), 0),
        "value_matrix": noise(key_list[2], (PACKED_TOKENS, KEY_VALUE_HEADS * HEAD_SIZE), 1.0, 6.0, ((0, 128),)),
        "attention_output": noise(key_list[3], (PACKED_TOKENS, QUERY_HEADS * HEAD_SIZE), 1.0, 6.0, ((0, 128),)),
        "output_gradient": noise(key_list[4], (PACKED_TOKENS, QUERY_HEADS * HEAD_SIZE), 1.0, 6.0, ((0, 128),)),
        "lengths": uneven(key_list[5], DOCS, PACKED_TOKENS, MOST, 2).astype(jnp.int32),
    }


NEG = -1.0e30


def document_index(positions, lengths):
    starts = jnp.cumsum(lengths, dtype=jnp.int32) - lengths
    starts_hit = (starts[None, :] <= positions[:, None]).astype(jnp.int32)
    return jnp.sum(starts_hit, axis=1).astype(jnp.int32) - 1


def reference(queries, key_matrix, value_matrix, attention_output, output_gradient, lengths):
    query_group_width = QUERY_HEADS // KEY_VALUE_HEADS
    window_len = (REACH + 1) * T_DEV
    leading_padding = REACH * T_DEV
    inv_root = HEAD_SIZE ** -0.5
    query_gathered = queries.reshape(PACKED_TOKENS, KEY_VALUE_HEADS, query_group_width, HEAD_SIZE)
    output_grad_gathered = output_gradient.reshape(PACKED_TOKENS, KEY_VALUE_HEADS, query_group_width, HEAD_SIZE)
    output_gathered = attention_output.reshape(PACKED_TOKENS, KEY_VALUE_HEADS, query_group_width, HEAD_SIZE)
    key_padded = jnp.concatenate([jnp.zeros((leading_padding, KEY_VALUE_HEADS, HEAD_SIZE), key_matrix.dtype), key_matrix.reshape(PACKED_TOKENS, KEY_VALUE_HEADS, HEAD_SIZE)], axis=0)
    value_padded = jnp.concatenate([jnp.zeros((leading_padding, KEY_VALUE_HEADS, HEAD_SIZE), value_matrix.dtype), value_matrix.reshape(PACKED_TOKENS, KEY_VALUE_HEADS, HEAD_SIZE)], axis=0)

    def block_step(state, block_index):
        key_grad_accum, value_grad_accum = state
        block_start = block_index * T_DEV
        q_blk = lax.dynamic_slice_in_dim(query_gathered, block_start, T_DEV, 0).astype(jnp.float32)
        g_blk = lax.dynamic_slice_in_dim(output_grad_gathered, block_start, T_DEV, 0).astype(jnp.float32)
        o_blk = lax.dynamic_slice_in_dim(output_gathered, block_start, T_DEV, 0).astype(jnp.float32)
        k_blk = lax.dynamic_slice_in_dim(key_padded, block_start, window_len, 0).astype(jnp.float32)
        v_blk = lax.dynamic_slice_in_dim(value_padded, block_start, window_len, 0).astype(jnp.float32)
        q_pos = block_start + jnp.arange(T_DEV, dtype=jnp.int32)
        k_pos = block_start - leading_padding + jnp.arange(window_len, dtype=jnp.int32)
        allowed = (document_index(q_pos, lengths)[:, None] == document_index(k_pos, lengths)[None, :]) & (k_pos[None, :] <= q_pos[:, None])
        scores = jnp.einsum("ikgd,jkd->kgij", q_blk, k_blk) * inv_root
        masked = jnp.where(allowed, scores, NEG)
        row_top = jnp.max(masked, axis=-1, keepdims=True)
        row_total = jnp.sum(jnp.where(allowed, jnp.exp(masked - row_top), 0.0), axis=-1, keepdims=True)
        log_total = row_top + jnp.log(row_total)
        probs = jnp.where(allowed, jnp.exp(masked - log_total), 0.0)
        probs_low = lax.optimization_barrier(probs.astype(jnp.bfloat16)).astype(jnp.float32)
        row_delta = jnp.einsum("ikgd,ikgd->kgi", g_blk, o_blk)[..., None]
        dprobs = jnp.einsum("ikgd,jkd->kgij", g_blk, v_blk)
        dscores = probs * (dprobs - row_delta)
        ds_low = lax.optimization_barrier(dscores.astype(jnp.bfloat16)).astype(jnp.float32)
        dq_blk = jnp.einsum("kgij,jkd->ikgd", ds_low, k_blk) * inv_root
        dk_win = jnp.einsum("kgij,ikgd->jkd", ds_low, q_blk) * inv_root
        dv_win = jnp.einsum("kgij,ikgd->jkd", probs_low, g_blk)
        key_grad_accum = lax.dynamic_update_slice_in_dim(key_grad_accum, lax.dynamic_slice_in_dim(key_grad_accum, block_start, window_len, 0) + dk_win, block_start, 0)
        value_grad_accum = lax.dynamic_update_slice_in_dim(value_grad_accum, lax.dynamic_slice_in_dim(value_grad_accum, block_start, window_len, 0) + dv_win, block_start, 0)
        return (key_grad_accum, value_grad_accum), dq_blk.astype(jnp.bfloat16)

    empty_accumulator = jnp.zeros((leading_padding + PACKED_TOKENS, KEY_VALUE_HEADS, HEAD_SIZE), jnp.float32)
    (key_grad_accum, value_grad_accum), dq_blocks = lax.scan(block_step, (empty_accumulator, empty_accumulator), jnp.arange(PACKED_TOKENS // T_DEV, dtype=jnp.int32))
    query_grad = dq_blocks.reshape(PACKED_TOKENS, QUERY_HEADS * HEAD_SIZE)
    key_gradient = key_grad_accum[leading_padding:].astype(jnp.bfloat16).reshape(PACKED_TOKENS, KEY_VALUE_HEADS * HEAD_SIZE)
    value_gradient = value_grad_accum[leading_padding:].astype(jnp.bfloat16).reshape(PACKED_TOKENS, KEY_VALUE_HEADS * HEAD_SIZE)
    return query_grad, key_gradient, value_gradient
```

```python
import functools
import math

import jax
import jax.numpy as jnp
from jax import lax
from jax.experimental import pallas as pl
from jax.experimental.pallas import tpu as pltpu
from jax.sharding import PartitionSpec as P

HEAD_SIZE = 128
SHARD = 256
HALF = 128
SLOTS = 8
ROW = 4
NEG = -1e30
MESH = pl.DeviceIdType.MESH
F32 = jnp.float32
BF16 = jnp.bfloat16


def dot_nt(a, b):
    return lax.dot_general(a, b, (((1,), (1,)), ((), ())), preferred_element_type=F32)


def dot_nn(a, b):
    return jnp.dot(a, b, preferred_element_type=F32)


def kernel(
    n_ctx,
    n_kv,
    width,
    q_in,
    k_in,
    v_in,
    o_in,
    g_in,
    len_ref,
    dq_out,
    dk_out,
    dv_out,
    qgo,
    kv,
    ebuf,
    bias,
    mx,
    zs,
    delta,
    dqt,
    acc,
    ret_out,
    ret_in,
    dq_stage,
    dkv_stage,
    sem_qgo_l,
    sem_qgo_s,
    sem_qgo_r,
    sem_kv0_l,
    sem_kv0_s,
    sem_kv0_r,
    sem_kv_s,
    sem_kv_r,
    sem_ret_s,
    sem_ret_r,
    sem_dq_l,
    sem_dq_s,
    sem_dq_r,
    sem_dkv_l,
    sem_dkv_s,
    sem_dkv_r,
):
    ctx = lax.axis_index("ctx")
    tp = lax.axis_index("tp")
    x = lax.rem(ctx, ROW)
    row = ctx - x
    other = 1 - tp
    up = lax.rem(ctx + ROW, n_ctx)
    down = lax.rem(ctx + n_ctx - ROW, n_ctx)
    wide = width * HEAD_SIZE
    inv_root = HEAD_SIZE ** -0.5
    to_exp2 = inv_root * math.log2(math.e)

    def along(d):
        return row + lax.rem(x + d, ROW)

    barrier = pltpu.get_barrier_semaphore()
    for peer in [(ctx, other), (up, tp), (down, tp)] + [(along(d), tp) for d in (1, 2, 3)]:
        pl.semaphore_signal(barrier, inc=1, device_id=peer, device_id_type=MESH)
    pl.semaphore_wait(barrier, 6)

    def cols(head, size):
        return pl.ds(pl.multiple_of(head * size, size), size)

    mine = pl.ds(pl.multiple_of(tp * HALF, HALF), HALF)
    theirs = pl.ds(pl.multiple_of(other * HALF, HALF), HALF)
    wides = (q_in, g_in, o_in)
    narrows = (k_in, v_in)

    def wide_local(a, g):
        return pltpu.make_async_copy(
            wides[a].at[:, cols(tp * n_kv + g, wide)], qgo.at[a, g, mine], sem_qgo_l.at[a, g])

    def wide_remote(a, g):
        return pltpu.make_async_remote_copy(
            wides[a].at[:, cols(other * n_kv + g, wide)], qgo.at[a, g, mine],
            sem_qgo_s.at[a, g], sem_qgo_r.at[a, g], device_id=(ctx, other), device_id_type=MESH)

    def narrow_local(a, g):
        return pltpu.make_async_copy(
            narrows[a].at[:, cols(tp * n_kv + g, HEAD_SIZE)], kv.at[a, g, 0, mine], sem_kv0_l.at[a, g])

    def narrow_remote(a, g):
        return pltpu.make_async_remote_copy(
            narrows[a].at[:, cols(other * n_kv + g, HEAD_SIZE)], kv.at[a, g, 0, mine],
            sem_kv0_s.at[a, g], sem_kv0_r.at[a, g], device_id=(ctx, other), device_id_type=MESH)

    def kv_y(a, g, d):
        return pltpu.make_async_remote_copy(
            kv.at[a, g, d], kv.at[a, g, ROW + d],
            sem_kv_s.at[a, g, ROW + d], sem_kv_r.at[a, g, ROW + d], device_id=(up, tp), device_id_type=MESH)

    def kv_x(a, g, d):
        held = ROW * ((x + d) // ROW)
        return pltpu.make_async_remote_copy(
            kv.at[a, g, held], kv.at[a, g, d],
            sem_kv_s.at[a, g, d], sem_kv_r.at[a, g, d], device_id=(along(d), tp), device_id_type=MESH)

    def ret_y(g, slot):
        return pltpu.make_async_remote_copy(
            ret_out.at[g, slot], ret_in.at[g, slot],
            sem_ret_s.at[g, slot], sem_ret_r.at[g, slot], device_id=(down, tp), device_id_type=MESH)

    def ret_x(g, d):
        return pltpu.make_async_remote_copy(
            ret_out.at[g, d], ret_in.at[g, d],
            sem_ret_s.at[g, d], sem_ret_r.at[g, d], device_id=(along(ROW - d), tp), device_id_type=MESH)

    def dq_local(g):
        return pltpu.make_async_copy(
            dq_stage.at[g, mine], dq_out.at[:, cols(tp * n_kv + g, wide)], sem_dq_l.at[g])

    def dq_remote(g):
        return pltpu.make_async_remote_copy(
            dq_stage.at[g, theirs], dq_out.at[:, cols(tp * n_kv + g, wide)],
            sem_dq_s.at[g], sem_dq_r.at[g], device_id=(ctx, other), device_id_type=MESH)

    dkvs = (dk_out, dv_out)

    def dkv_local(a, g):
        return pltpu.make_async_copy(
            dkv_stage.at[g, a, mine], dkvs[a].at[:, cols(tp * n_kv + g, HEAD_SIZE)], sem_dkv_l.at[a, g])

    def dkv_remote(a, g):
        return pltpu.make_async_remote_copy(
            dkv_stage.at[g, a, theirs], dkvs[a].at[:, cols(tp * n_kv + g, HEAD_SIZE)],
            sem_dkv_s.at[a, g], sem_dkv_r.at[a, g], device_id=(ctx, other), device_id_type=MESH)

    for g in range(n_kv):
        for a in (0, 1):
            narrow_remote(a, g).start()
            narrow_local(a, g).start()
        if g == 0:
            wide_remote(0, 0).start()
            wide_local(0, 0).start()
    for g in range(n_kv):
        for a in (0, 1, 2):
            if (a, g) != (0, 0):
                wide_remote(a, g).start()
                wide_local(a, g).start()

    first = (ctx * SHARD).astype(F32)
    docs = len_ref.shape[1]
    lens = len_ref[...].astype(F32)
    r_d = lax.broadcasted_iota(jnp.int32, (docs, docs), 0)
    c_d = lax.broadcasted_iota(jnp.int32, (docs, docs), 1)
    starts = jnp.sum(jnp.where(c_d < r_d, jnp.broadcast_to(lens, (docs, docs)), 0.0), axis=1, keepdims=True)
    pos = lax.broadcasted_iota(jnp.int32, (docs, SHARD), 1).astype(F32) + first
    begin = jnp.max(jnp.where(starts <= pos, jnp.broadcast_to(starts, (docs, SHARD)), 0.0), axis=0, keepdims=True)
    q_row = lax.broadcasted_iota(jnp.int32, (SHARD, SHARD), 1).astype(F32) + first
    k_row = lax.broadcasted_iota(jnp.int32, (SHARD, SHARD), 0).astype(F32) + first

    def write_bias(s, carry):
        k_pos = k_row - (s * SHARD).astype(F32)
        keep = (k_pos >= begin) & (k_pos <= q_row)
        bias[s] = jnp.where(keep, 0.0, NEG)
        return carry

    lax.fori_loop(0, SLOTS, write_bias, 0)

    for g in range(n_kv):
        for a in (0, 1):
            narrow_local(a, g).wait()
            narrow_remote(a, g).wait_recv()
            kv_y(a, g, 0).start()

    def forward_x(g):
        for a in (0, 1):
            kv_y(a, g, 0).wait_recv()
        for a in (0, 1):
            for d in (1, 2, 3):
                kv_x(a, g, d).start()

    def forward_y(g, d):
        for a in (0, 1):
            kv_x(a, g, d).wait_recv()
            kv_y(a, g, d).start()

    def back_x(g):
        par = lax.rem(g, 2)

        def one(d, carry):
            ret_y(g, ROW + d).wait_recv()
            ret_out[g, d] = (acc[par, d] + ret_in[g, ROW + d].astype(F32)).astype(BF16)
            ret_x(g, d).start()
            return carry

        lax.fori_loop(1, ROW, one, 0)

    def back_y(g):
        par = lax.rem(g, 2)
        far = acc[par, ROW]
        near = acc[par, 0]
        for d in (1, 2, 3):
            ret_x(g, d).wait_recv()
            part = ret_in[g, d].astype(F32)
            crosses = ((x + d) // ROW).astype(F32)
            far = far + part * crosses
            near = near + part * (1.0 - crosses)
        ret_out[g, ROW] = far.astype(BF16)
        ret_y(g, ROW).start()
        acc[par, 0] = near

    def back_end(g):
        par = lax.rem(g, 2)
        ret_y(g, ROW).wait_recv()
        total = (acc[par, 0] + ret_in[g, ROW].astype(F32)).astype(BF16)
        dkv_stage[g] = total
        for a in (0, 1):
            dkv_remote(a, g).start()
            dkv_local(a, g).start()

    def head_cols(h):
        return slice(h * HEAD_SIZE, (h + 1) * HEAD_SIZE)

    def phase_a(g, s):
        keys = kv[0, g, s]
        tops, sums = [], []
        for h in range(width):
            sc = dot_nt(keys, qgo[0, g, :, head_cols(h)])
            sc = sc * to_exp2 + bias[s]
            top = jnp.max(sc, axis=0, keepdims=True)
            e = jnp.exp2(sc - top)
            ebuf[s, h] = e
            tops.append(top)
            sums.append(jnp.sum(e, axis=0, keepdims=True))
        mx[s] = jnp.concatenate(tops, axis=0)
        zs[s] = jnp.concatenate(sums, axis=0)

    def normalise(g):
        top = mx[0]
        for s in range(1, SLOTS):
            top = jnp.maximum(top, mx[s])
        total = jnp.zeros_like(top)
        for s in range(SLOTS):
            f = jnp.exp2(mx[s] - top)
            total = total + zs[s] * f
            mx[s] = f
        inv = 1.0 / total
        for s in range(SLOTS):
            mx[s] = mx[s] * inv
        ones = jnp.ones((8, 2 * HEAD_SIZE), BF16)
        for h in range(width):
            prod = qgo[1, g, :, head_cols(h)].astype(F32) * qgo[2, g, :, head_cols(h)].astype(F32)
            hi = prod.astype(BF16)
            lo = (prod - hi.astype(F32)).astype(BF16)
            delta[h : h + 1] = dot_nt(ones, jnp.concatenate([hi, lo], axis=1))[0:1]
        dqt[...] = jnp.zeros_like(dqt)

    def phase_b(g, s):
        keys = kv[0, g, s]
        values = kv[1, g, s]
        keys_t = keys.T
        f = mx[s]
        dk = jnp.zeros((SHARD, HEAD_SIZE), F32)
        dv = jnp.zeros((SHARD, HEAD_SIZE), F32)
        for h in range(width):
            q_h = qgo[0, g, :, head_cols(h)]
            g_h = qgo[1, g, :, head_cols(h)]
            p = ebuf[s, h] * f[h : h + 1]
            dp = dot_nt(values, g_h)
            ds = (p * (dp - delta[h : h + 1])).astype(BF16)
            dv = dv + dot_nn(p.astype(BF16), g_h)
            dk = dk + dot_nn(ds, q_h)
            dqt[h] += dot_nn(keys_t, ds)
        return dk * inv_root, dv

    def finish_dq(g):
        for h in range(width):
            dq_stage[g, :, head_cols(h)] = (dqt[h].T * inv_root).astype(BF16)
        dq_remote(g).start()
        dq_local(g).start()

    def head_step(g, carry):
        par = lax.rem(g, 2)
        wide_local(0, g).wait()
        wide_remote(0, g).wait_recv()

        def a_step(i, carry_a):
            s = lax.select(i == 0, 0, lax.select(i == 1, ROW, lax.select(i < 5, i - 1, i)))

            @pl.when((g == 0) & (i == 1))
            def _():
                forward_x(g)

            @pl.when((g == 0) & (i >= 2) & (i < 5))
            def _():
                forward_y(g, i - 1)

            @pl.when(i >= 5)
            def _():
                kv_y(0, g, i - ROW).wait_recv()

            @pl.when((g > 0) & (i == 5))
            def _():
                back_x(g - 1)

            phase_a(g, s)
            return carry_a

        lax.fori_loop(0, SLOTS, a_step, 0)

        for a in (1, 2):
            wide_local(a, g).wait()
            wide_remote(a, g).wait_recv()
        normalise(g)

        def b_step(i, carry_b):
            s = lax.select(i < 3, i + 5, lax.rem(i + 3, 5))

            @pl.when(i < 3)
            def _():
                kv_y(1, g, i + 1).wait_recv()

            @pl.when((g < n_kv - 1) & (i == 0))
            def _():
                forward_x(g + 1)

            @pl.when((g < n_kv - 1) & (i >= 3) & (i < 6))
            def _():
                forward_y(g + 1, i - 2)

            @pl.when((g > 0) & (i == 2))
            def _():
                back_y(g - 1)

            @pl.when((g > 0) & (i == 7))
            def _():
                back_end(g - 1)

            dk, dv = phase_b(g, s)

            @pl.when(i < 3)
            def _():
                ret_out[g, s, 0] = dk.astype(BF16)
                ret_out[g, s, 1] = dv.astype(BF16)
                ret_y(g, s).start()

            @pl.when(i >= 3)
            def _():
                acc[par, s, 0] = dk
                acc[par, s, 1] = dv

            return carry_b

        lax.fori_loop(0, SLOTS, b_step, 0)
        finish_dq(g)
        return carry

    lax.fori_loop(0, n_kv, head_step, 0)
    last = jnp.int32(n_kv - 1)
    back_x(last)
    back_y(last)
    back_end(last)

    def drain(g, carry):
        for a in (0, 1, 2):
            wide_remote(a, g).wait_send()
        for a in (0, 1):
            narrow_remote(a, g).wait_send()
            for d in range(ROW):
                kv_y(a, g, d).wait_send()
            for d in (1, 2, 3):
                kv_x(a, g, d).wait_send()
            dkv_local(a, g).wait()
            dkv_remote(a, g).wait()
        for s in range(ROW, SLOTS):
            ret_y(g, s).wait_send()
        for d in (1, 2, 3):
            ret_x(g, d).wait_send()
        dq_local(g).wait()
        dq_remote(g).wait()
        return carry

    lax.fori_loop(0, n_kv, drain, 0)


def per_device(queries, key_matrix, value_matrix, attention_output, output_gradient, lengths):
    n_ctx = lax.axis_size("ctx")
    n_tp = lax.axis_size("tp")
    heads_q = queries.shape[1] // HEAD_SIZE
    heads_kv = key_matrix.shape[1] // HEAD_SIZE
    n_kv = heads_kv // n_tp
    width = heads_q // heads_kv
    wide = width * HEAD_SIZE
    dma = pltpu.SemaphoreType.DMA
    flops = 5 * 2 * SHARD * SLOTS * SHARD * HEAD_SIZE * n_kv * width
    return pl.pallas_call(
        functools.partial(kernel, n_ctx, n_kv, width),
        out_shape=(
            jax.ShapeDtypeStruct(queries.shape, BF16),
            jax.ShapeDtypeStruct(key_matrix.shape, BF16),
            jax.ShapeDtypeStruct(value_matrix.shape, BF16),
        ),
        in_specs=[pl.BlockSpec(memory_space=pl.ANY)] * 5 + [pl.BlockSpec(memory_space=pltpu.VMEM)],
        out_specs=(pl.BlockSpec(memory_space=pl.ANY),) * 3,
        scratch_shapes=[
            pltpu.VMEM((3, n_kv, SHARD, wide), BF16),
            pltpu.VMEM((2, n_kv, SLOTS, SHARD, HEAD_SIZE), BF16),
            pltpu.VMEM((SLOTS, width, SHARD, SHARD), F32),
            pltpu.VMEM((SLOTS, SHARD, SHARD), F32),
            pltpu.VMEM((SLOTS, width, SHARD), F32),
            pltpu.VMEM((SLOTS, width, SHARD), F32),
            pltpu.VMEM((width, SHARD), F32),
            pltpu.VMEM((width, HEAD_SIZE, SHARD), F32),
            pltpu.VMEM((2, ROW + 1, 2, SHARD, HEAD_SIZE), F32),
            pltpu.VMEM((n_kv, SLOTS, 2, SHARD, HEAD_SIZE), BF16),
            pltpu.VMEM((n_kv, SLOTS, 2, SHARD, HEAD_SIZE), BF16),
            pltpu.VMEM((n_kv, SHARD, wide), BF16),
            pltpu.VMEM((n_kv, 2, SHARD, HEAD_SIZE), BF16),
            dma((3, n_kv)),
            dma((3, n_kv)),
            dma((3, n_kv)),
            dma((2, n_kv)),
            dma((2, n_kv)),
            dma((2, n_kv)),
            dma((2, n_kv, SLOTS)),
            dma((2, n_kv, SLOTS)),
            dma((n_kv, SLOTS)),
            dma((n_kv, SLOTS)),
            dma((n_kv,)),
            dma((n_kv,)),
            dma((n_kv,)),
            dma((2, n_kv)),
            dma((2, n_kv)),
            dma((2, n_kv)),
        ],
        compiler_params=pltpu.CompilerParams(
            collective_id=0, has_side_effects=True, vmem_limit_bytes=60 * 1024 * 1024
        ),
        cost_estimate=pl.CostEstimate(
            flops=flops, bytes_accessed=10 * 1024 * 1024, transcendentals=flops // (10 * HEAD_SIZE)
        ),
        name="attention_backward",
    )(
        queries,
        key_matrix,
        value_matrix,
        attention_output,
        output_gradient,
        lengths.reshape(1, lengths.shape[0]),
    )


def solution(mesh):
    rows = P(("ctx", "tp"), None)
    return jax.shard_map(
        per_device,
        mesh=mesh,
        in_specs=(rows, rows, rows, rows, rows, P()),
        out_specs=(rows, rows, rows),
        check_vma=False,
    )
```

```python
import functools
import math

import jax
import jax.numpy as jnp
from jax import lax
from jax.experimental import pallas as pl
from jax.experimental.pallas import tpu as pltpu
from jax.sharding import PartitionSpec as P

HEAD_SIZE = 128
SHARD = 256
HALF = 128
SLOTS = 8
ROW = 4
NEG = -1e30
MESH = pl.DeviceIdType.MESH
F32 = jnp.float32
BF16 = jnp.bfloat16


def dot_nt(a, b):
    return lax.dot_general(a, b, (((1,), (1,)), ((), ())), preferred_element_type=F32)


def dot_nn(a, b):
    return jnp.dot(a, b, preferred_element_type=F32)


def kernel(
    n_ctx,
    n_kv,
    width,
    q_in,
    k_in,
    v_in,
    o_in,
    g_in,
    len_ref,
    dq_out,
    dk_out,
    dv_out,
    qgo,
    kv,
    sbuf,
    bias,
    tops,
    invs,
    deltas,
    q_t,
    g_t,
    probs,
    dsc,
    acc,
    ret_out,
    ret_in,
    dq_stage,
    dkv_stage,
    sem_qgo_l,
    sem_qgo_s,
    sem_qgo_r,
    sem_kv0_l,
    sem_kv0_s,
    sem_kv0_r,
    sem_kv_s,
    sem_kv_r,
    sem_ret_s,
    sem_ret_r,
    sem_dq_l,
    sem_dq_s,
    sem_dq_r,
    sem_dkv_l,
    sem_dkv_s,
    sem_dkv_r,
):
    ctx = lax.axis_index("ctx")
    tp = lax.axis_index("tp")
    x = lax.rem(ctx, ROW)
    row = ctx - x
    other = 1 - tp
    up = lax.rem(ctx + ROW, n_ctx)
    down = lax.rem(ctx + n_ctx - ROW, n_ctx)
    wide = width * HEAD_SIZE
    inv_root = HEAD_SIZE ** -0.5
    to_exp2 = inv_root * math.log2(math.e)

    def along(d):
        return row + lax.rem(x + d, ROW)

    barrier = pltpu.get_barrier_semaphore()
    for peer in [(ctx, other), (up, tp), (down, tp)] + [(along(d), tp) for d in (1, 2, 3)]:
        pl.semaphore_signal(barrier, inc=1, device_id=peer, device_id_type=MESH)
    pl.semaphore_wait(barrier, 6)

    def cols(head, size):
        return pl.ds(pl.multiple_of(head * size, size), size)

    mine = pl.ds(pl.multiple_of(tp * HALF, HALF), HALF)
    theirs = pl.ds(pl.multiple_of(other * HALF, HALF), HALF)
    wides = (q_in, g_in, o_in)
    narrows = (k_in, v_in)

    def wide_local(a, g):
        return pltpu.make_async_copy(
            wides[a].at[:, cols(tp * n_kv + g, wide)], qgo.at[a, g, mine], sem_qgo_l.at[a, g])

    def wide_remote(a, g):
        return pltpu.make_async_remote_copy(
            wides[a].at[:, cols(other * n_kv + g, wide)], qgo.at[a, g, mine],
            sem_qgo_s.at[a, g], sem_qgo_r.at[a, g], device_id=(ctx, other), device_id_type=MESH)

    def narrow_local(a, g):
        return pltpu.make_async_copy(
            narrows[a].at[:, cols(tp * n_kv + g, HEAD_SIZE)], kv.at[a, g, 0, mine], sem_kv0_l.at[a, g])

    def narrow_remote(a, g):
        return pltpu.make_async_remote_copy(
            narrows[a].at[:, cols(other * n_kv + g, HEAD_SIZE)], kv.at[a, g, 0, mine],
            sem_kv0_s.at[a, g], sem_kv0_r.at[a, g], device_id=(ctx, other), device_id_type=MESH)

    def kv_y(a, g, d):
        return pltpu.make_async_remote_copy(
            kv.at[a, g, d], kv.at[a, g, ROW + d],
            sem_kv_s.at[a, g, ROW + d], sem_kv_r.at[a, g, ROW + d], device_id=(up, tp), device_id_type=MESH)

    def kv_x(a, g, d):
        held = ROW * ((x + d) // ROW)
        return pltpu.make_async_remote_copy(
            kv.at[a, g, held], kv.at[a, g, d],
            sem_kv_s.at[a, g, d], sem_kv_r.at[a, g, d], device_id=(along(d), tp), device_id_type=MESH)

    def ret_y(g, slot):
        return pltpu.make_async_remote_copy(
            ret_out.at[g, slot], ret_in.at[g, slot],
            sem_ret_s.at[g, slot], sem_ret_r.at[g, slot], device_id=(down, tp), device_id_type=MESH)

    def ret_x(g, d):
        return pltpu.make_async_remote_copy(
            ret_out.at[g, d], ret_in.at[g, d],
            sem_ret_s.at[g, d], sem_ret_r.at[g, d], device_id=(along(ROW - d), tp), device_id_type=MESH)

    def dq_local(g):
        return pltpu.make_async_copy(
            dq_stage.at[g, mine], dq_out.at[:, cols(tp * n_kv + g, wide)], sem_dq_l.at[g])

    def dq_remote(g):
        return pltpu.make_async_remote_copy(
            dq_stage.at[g, theirs], dq_out.at[:, cols(tp * n_kv + g, wide)],
            sem_dq_s.at[g], sem_dq_r.at[g], device_id=(ctx, other), device_id_type=MESH)

    dkvs = (dk_out, dv_out)

    def dkv_local(a, g):
        return pltpu.make_async_copy(
            dkv_stage.at[g, a, mine], dkvs[a].at[:, cols(tp * n_kv + g, HEAD_SIZE)], sem_dkv_l.at[a, g])

    def dkv_remote(a, g):
        return pltpu.make_async_remote_copy(
            dkv_stage.at[g, a, theirs], dkvs[a].at[:, cols(tp * n_kv + g, HEAD_SIZE)],
            sem_dkv_s.at[a, g], sem_dkv_r.at[a, g], device_id=(ctx, other), device_id_type=MESH)

    def begin_narrow(g):
        for a in (0, 1):
            narrow_remote(a, g).start()
            narrow_local(a, g).start()

    def begin_wide(a, g):
        wide_remote(a, g).start()
        wide_local(a, g).start()

    def forward_first(g):
        for a in (0, 1):
            narrow_local(a, g).wait()
            narrow_remote(a, g).wait_recv()
            kv_y(a, g, 0).start()

    begin_narrow(0)
    begin_wide(0, 0)
    for g in range(1, n_kv):
        begin_narrow(g)
    for g in range(n_kv):
        for a in (0, 1, 2):
            if (a, g) != (0, 0):
                begin_wide(a, g)
    forward_first(0)
    forward_first(1)

    first = (ctx * SHARD).astype(F32)
    docs = len_ref.shape[1]
    lens = len_ref[...].astype(F32)
    r_d = lax.broadcasted_iota(jnp.int32, (docs, docs), 0)
    c_d = lax.broadcasted_iota(jnp.int32, (docs, docs), 1)
    starts = jnp.sum(jnp.where(c_d < r_d, jnp.broadcast_to(lens, (docs, docs)), 0.0), axis=1, keepdims=True)
    pos = lax.broadcasted_iota(jnp.int32, (docs, SHARD), 1).astype(F32) + first
    begin = jnp.max(jnp.where(starts <= pos, jnp.broadcast_to(starts, (docs, SHARD)), 0.0), axis=0, keepdims=True)
    begin = jnp.broadcast_to(begin, (SHARD, SHARD)).T
    q_row = lax.broadcasted_iota(jnp.int32, (SHARD, SHARD), 0).astype(F32) + first
    k_row = lax.broadcasted_iota(jnp.int32, (SHARD, SHARD), 1).astype(F32) + first

    def write_bias(s, carry):
        k_pos = k_row - (s * SHARD).astype(F32)
        keep = (k_pos >= begin) & (k_pos <= q_row)
        bias[s] = jnp.where(keep, 0.0, NEG)
        return carry

    lax.fori_loop(0, SLOTS, write_bias, 0)
    dsc[...] = jnp.zeros_like(dsc)

    def forward_x(g):
        for a in (0, 1):
            kv_y(a, g, 0).wait_recv()
            for d in (1, 3, 2):
                kv_x(a, g, d).start()

    def forward_y(g, d):
        for a in (0, 1):
            kv_x(a, g, d).wait_recv()
            kv_y(a, g, d).start()

    def back_x(g):
        par = lax.rem(g, 2)

        def one(d, carry):
            ret_y(g, ROW + d).wait_recv()
            ret_out[g, d] = (acc[par, d] + ret_in[g, ROW + d].astype(F32)).astype(BF16)
            ret_x(g, d).start()
            return carry

        lax.fori_loop(1, ROW, one, 0)

    def back_y(g):
        par = lax.rem(g, 2)
        far = acc[par, ROW]
        near = acc[par, 0]
        for d in (1, 2, 3):
            ret_x(g, d).wait_recv()
            part = ret_in[g, d].astype(F32)
            crosses = ((x + d) // ROW).astype(F32)
            far = far + part * crosses
            near = near + part * (1.0 - crosses)
        ret_out[g, ROW] = far.astype(BF16)
        ret_y(g, ROW).start()
        acc[par, 0] = near

    def back_end(g):
        par = lax.rem(g, 2)
        ret_y(g, ROW).wait_recv()
        for a in (0, 1):
            total = acc[par, 0, a] + ret_in[g, ROW, a].astype(F32)
            dkv_stage[g, a] = total.T.astype(BF16)
            dkv_remote(a, g).start()
            dkv_local(a, g).start()

    def lanes(h, size):
        return pl.ds(pl.multiple_of(h * size, size), size)

    def head_cols(h):
        return slice(h * HEAD_SIZE, (h + 1) * HEAD_SIZE)

    def head_rows(h):
        return slice(h * SHARD, (h + 1) * SHARD)

    def twice(t):
        return jnp.concatenate([t, t], axis=1)

    def scores_step(g, s):
        keys_t = kv[0, g, s].T
        for h in range(width):
            sc = dot_nn(qgo[0, g, :, head_cols(h)], keys_t)
            sc = sc * to_exp2 + bias[s]
            sbuf[s, h] = sc
            tops[h] = jnp.maximum(tops[h], jnp.maximum(sc[:, :HEAD_SIZE], sc[:, HEAD_SIZE:]))

    def dq_head(g, h):
        left = jnp.concatenate([dsc[s, lanes(h, SHARD)] for s in range(SLOTS)], axis=1)
        right = kv[0, g].reshape(SLOTS * SHARD, HEAD_SIZE)
        dq_stage[g, :, lanes(h, HEAD_SIZE)] = (dot_nn(left, right) * inv_root).astype(BF16)

    def softmax_head(g, h):
        q_h = qgo[0, g, :, lanes(h, HEAD_SIZE)]
        g_h = qgo[1, g, :, lanes(h, HEAD_SIZE)]
        o_h = qgo[2, g, :, lanes(h, HEAD_SIZE)]
        q_t[:, lanes(h, SHARD)] = q_h.T
        g_t[:, lanes(h, SHARD)] = g_h.T
        delta = jnp.sum(g_h.astype(F32) * o_h.astype(F32), axis=1, keepdims=True)
        deltas[h] = jnp.broadcast_to(delta, (SHARD, HEAD_SIZE))
        top = jnp.max(tops[h], axis=1, keepdims=True)
        total = jnp.zeros((SHARD, HEAD_SIZE), F32)
        for s in range(SLOTS):
            e = jnp.exp2(sbuf[s, h] - top)
            sbuf[s, h] = e
            total = total + (e[:, :HEAD_SIZE] + e[:, HEAD_SIZE:])
        total = jnp.sum(total, axis=1, keepdims=True)
        invs[h] = jnp.broadcast_to(1.0 / total, (SHARD, HEAD_SIZE))

    def grads_step(g, s):
        values_t = kv[1, g, s].T
        for h in range(width):
            g_h = qgo[1, g, :, head_cols(h)]
            p = sbuf[s, h] * twice(invs[h])
            dp = dot_nn(g_h, values_t)
            probs[head_rows(h)] = p.astype(BF16)
            dsc[s, head_rows(h)] = (p * (dp - twice(deltas[h]))).astype(BF16)
        dk = dot_nn(q_t[...], dsc[s]) * inv_root
        dv = dot_nn(g_t[...], probs[...])
        return dk, dv

    def send_dq(g):
        dq_remote(g).start()
        dq_local(g).start()

    def head_step(g, carry):
        par = lax.rem(g, 2)
        before = jnp.maximum(g - 1, 0)
        wide_local(0, g).wait()
        wide_remote(0, g).wait_recv()
        tops[...] = jnp.full(tops.shape, 2 * NEG, F32)

        def scores_of(i, carry_a):
            s = lax.select(i == 0, 0, lax.select(i == 1, ROW, lax.select(i < 5, i - 1, i)))

            @pl.when((g == 0) & (i == 1))
            def _():
                forward_x(g)

            @pl.when((g == 0) & (i >= 2) & (i < 5))
            def _():
                forward_y(g, i - 1)

            @pl.when((g == 0) & (i == 5))
            def _():
                forward_x(1)
                for later in range(2, n_kv):
                    forward_first(later)

            @pl.when((g > 1) & (i == 0))
            def _():
                back_y(g - 2)

            @pl.when(i >= 5)
            def _():
                kv_y(0, g, i - ROW).wait_recv()

            scores_step(g, s)
            return carry_a

        lax.fori_loop(0, SLOTS, scores_of, 0)

        for a in (1, 2):
            wide_local(a, g).wait()
            wide_remote(a, g).wait_recv()

        def softmax_of(h, carry_s):
            dq_head(before, h)
            softmax_head(g, h)
            return carry_s

        lax.fori_loop(0, width, softmax_of, 0)

        @pl.when(g > 0)
        def _():
            send_dq(g - 1)

        def grads_of(i, carry_b):
            s = lax.select(i < 3, i + 5, lax.rem(i + 3, 5))

            @pl.when((g < n_kv - 1) & (i == 0))
            def _():
                for d in (1, 3, 2):
                    forward_y(g + 1, d)

            @pl.when((g < n_kv - 2) & (i == 4))
            def _():
                forward_x(g + 2)

            @pl.when((g > 0) & (i == 0))
            def _():
                back_x(g - 1)

            @pl.when((g > 1) & (i == 0))
            def _():
                back_end(g - 2)

            @pl.when(i < 3)
            def _():
                kv_y(1, g, i + 1).wait_recv()

            dk, dv = grads_step(g, s)

            @pl.when(i < 3)
            def _():
                ret_out[g, s, 0] = dk.astype(BF16)
                ret_out[g, s, 1] = dv.astype(BF16)
                ret_y(g, s).start()

            @pl.when(i >= 3)
            def _():
                acc[par, s, 0] = dk
                acc[par, s, 1] = dv

            return carry_b

        lax.fori_loop(0, SLOTS, grads_of, 0)
        return carry

    lax.fori_loop(0, n_kv, head_step, 0)
    last = jnp.int32(n_kv - 1)
    back_y(last - 1)
    back_x(last)

    def last_dq(h, carry):
        dq_head(last, h)
        return carry

    lax.fori_loop(0, width, last_dq, 0)
    send_dq(last)
    back_y(last)
    back_end(last - 1)
    back_end(last)

    def drain(g, carry):
        for a in (0, 1, 2):
            wide_remote(a, g).wait_send()
        for a in (0, 1):
            narrow_remote(a, g).wait_send()
            for d in range(ROW):
                kv_y(a, g, d).wait_send()
            for d in (1, 2, 3):
                kv_x(a, g, d).wait_send()
            dkv_local(a, g).wait()
            dkv_remote(a, g).wait()
        for s in range(ROW, SLOTS):
            ret_y(g, s).wait_send()
        for d in (1, 2, 3):
            ret_x(g, d).wait_send()
        dq_local(g).wait()
        dq_remote(g).wait()
        return carry

    lax.fori_loop(0, n_kv, drain, 0)


def per_device(queries, key_matrix, value_matrix, attention_output, output_gradient, lengths):
    n_ctx = lax.axis_size("ctx")
    n_tp = lax.axis_size("tp")
    heads_q = queries.shape[1] // HEAD_SIZE
    heads_kv = key_matrix.shape[1] // HEAD_SIZE
    n_kv = heads_kv // n_tp
    width = heads_q // heads_kv
    wide = width * HEAD_SIZE
    dma = pltpu.SemaphoreType.DMA
    flops = 5 * 2 * SHARD * SLOTS * SHARD * HEAD_SIZE * n_kv * width
    return pl.pallas_call(
        functools.partial(kernel, n_ctx, n_kv, width),
        out_shape=(
            jax.ShapeDtypeStruct(queries.shape, BF16),
            jax.ShapeDtypeStruct(key_matrix.shape, BF16),
            jax.ShapeDtypeStruct(value_matrix.shape, BF16),
        ),
        in_specs=[pl.BlockSpec(memory_space=pl.ANY)] * 5 + [pl.BlockSpec(memory_space=pltpu.VMEM)],
        out_specs=(pl.BlockSpec(memory_space=pl.ANY),) * 3,
        scratch_shapes=[
            pltpu.VMEM((3, n_kv, SHARD, wide), BF16),
            pltpu.VMEM((2, n_kv, SLOTS, SHARD, HEAD_SIZE), BF16),
            pltpu.VMEM((SLOTS, width, SHARD, SHARD), F32),
            pltpu.VMEM((SLOTS, SHARD, SHARD), F32),
            pltpu.VMEM((width, SHARD, HEAD_SIZE), F32),
            pltpu.VMEM((width, SHARD, HEAD_SIZE), F32),
            pltpu.VMEM((width, SHARD, HEAD_SIZE), F32),
            pltpu.VMEM((HEAD_SIZE, width * SHARD), BF16),
            pltpu.VMEM((HEAD_SIZE, width * SHARD), BF16),
            pltpu.VMEM((width * SHARD, SHARD), BF16),
            pltpu.VMEM((SLOTS, width * SHARD, SHARD), BF16),
            pltpu.VMEM((2, ROW + 1, 2, HEAD_SIZE, SHARD), F32),
            pltpu.VMEM((n_kv, SLOTS, 2, HEAD_SIZE, SHARD), BF16),
            pltpu.VMEM((n_kv, SLOTS, 2, HEAD_SIZE, SHARD), BF16),
            pltpu.VMEM((n_kv, SHARD, wide), BF16),
            pltpu.VMEM((n_kv, 2, SHARD, HEAD_SIZE), BF16),
            dma((3, n_kv)),
            dma((3, n_kv)),
            dma((3, n_kv)),
            dma((2, n_kv)),
            dma((2, n_kv)),
            dma((2, n_kv)),
            dma((2, n_kv, SLOTS)),
            dma((2, n_kv, SLOTS)),
            dma((n_kv, SLOTS)),
            dma((n_kv, SLOTS)),
            dma((n_kv,)),
            dma((n_kv,)),
            dma((n_kv,)),
            dma((2, n_kv)),
            dma((2, n_kv)),
            dma((2, n_kv)),
        ],
        compiler_params=pltpu.CompilerParams(
            collective_id=0, has_side_effects=True, vmem_limit_bytes=62 * 1024 * 1024
        ),
        cost_estimate=pl.CostEstimate(
            flops=flops, bytes_accessed=10 * 1024 * 1024, transcendentals=flops // (10 * HEAD_SIZE)
        ),
        name="attention_backward",
    )(
        queries,
        key_matrix,
        value_matrix,
        attention_output,
        output_gradient,
        lengths.reshape(1, lengths.shape[0]),
    )


def solution(mesh):
    rows = P(("ctx", "tp"), None)
    return jax.shard_map(
        per_device,
        mesh=mesh,
        in_specs=(rows, rows, rows, rows, rows, P()),
        out_specs=(rows, rows, rows),
        check_vma=False,
    )
```

```python
import functools
import math

import jax
import jax.numpy as jnp
from jax import lax
from jax.experimental import pallas as pl
from jax.experimental.pallas import tpu as pltpu
from jax.sharding import PartitionSpec as P

HEAD_SIZE = 128
SHARD = 256
HALF = 128
SLOTS = 8
ROW = 4
NEG = -1e30
MESH = pl.DeviceIdType.MESH
F32 = jnp.float32
BF16 = jnp.bfloat16


def dot_nt(a, b):
    return lax.dot_general(a, b, (((1,), (1,)), ((), ())), preferred_element_type=F32)


def dot_nn(a, b):
    return jnp.dot(a, b, preferred_element_type=F32)


def kernel(
    n_ctx,
    n_kv,
    width,
    q_in,
    k_in,
    v_in,
    o_in,
    g_in,
    len_ref,
    dq_out,
    dk_out,
    dv_out,
    qgo,
    kv,
    sbuf0,
    sbuf1,
    bias,
    tops0,
    tops1,
    k_t,
    invs,
    deltas,
    q_t,
    g_t,
    probs,
    dsc,
    acc,
    ret_out,
    ret_in,
    dq_stage,
    dkv_stage,
    sem_qgo_l,
    sem_qgo_s,
    sem_qgo_r,
    sem_kv0_l,
    sem_kv0_s,
    sem_kv0_r,
    sem_kv_s,
    sem_kv_r,
    sem_ret_s,
    sem_ret_r,
    sem_dq_l,
    sem_dq_s,
    sem_dq_r,
    sem_dkv_l,
    sem_dkv_s,
    sem_dkv_r,
):
    ctx = lax.axis_index("ctx")
    tp = lax.axis_index("tp")
    x = lax.rem(ctx, ROW)
    row = ctx - x
    other = 1 - tp
    up = lax.rem(ctx + ROW, n_ctx)
    down = lax.rem(ctx + n_ctx - ROW, n_ctx)
    wide = width * HEAD_SIZE
    inv_root = HEAD_SIZE ** -0.5
    to_exp2 = inv_root * math.log2(math.e)

    def along(d):
        return row + lax.rem(x + d, ROW)

    barrier = pltpu.get_barrier_semaphore()
    for peer in [(ctx, other), (up, tp), (down, tp)] + [(along(d), tp) for d in (1, 2, 3)]:
        pl.semaphore_signal(barrier, inc=1, device_id=peer, device_id_type=MESH)
    def cols(head, size):
        return pl.ds(pl.multiple_of(head * size, size), size)

    mine = pl.ds(pl.multiple_of(tp * HALF, HALF), HALF)
    theirs = pl.ds(pl.multiple_of(other * HALF, HALF), HALF)
    wides = (q_in, g_in, o_in)
    narrows = (k_in, v_in)

    def wide_local(a, g):
        return pltpu.make_async_copy(
            wides[a].at[:, cols(tp * n_kv + g, wide)], qgo.at[a, g, mine], sem_qgo_l.at[a, g])

    def wide_remote(a, g):
        return pltpu.make_async_remote_copy(
            wides[a].at[:, cols(other * n_kv + g, wide)], qgo.at[a, g, mine],
            sem_qgo_s.at[a, g], sem_qgo_r.at[a, g], device_id=(ctx, other), device_id_type=MESH)

    def narrow_local(a, g):
        return pltpu.make_async_copy(
            narrows[a].at[:, cols(tp * n_kv + g, HEAD_SIZE)], kv.at[a, g, 0, mine], sem_kv0_l.at[a, g])

    def narrow_remote(a, g):
        return pltpu.make_async_remote_copy(
            narrows[a].at[:, cols(other * n_kv + g, HEAD_SIZE)], kv.at[a, g, 0, mine],
            sem_kv0_s.at[a, g], sem_kv0_r.at[a, g], device_id=(ctx, other), device_id_type=MESH)

    def kv_y(a, g, d):
        return pltpu.make_async_remote_copy(
            kv.at[a, g, d], kv.at[a, g, ROW + d],
            sem_kv_s.at[a, g, ROW + d], sem_kv_r.at[a, g, ROW + d], device_id=(up, tp), device_id_type=MESH)

    def kv_x(a, g, d):
        held = ROW * ((x + d) // ROW)
        return pltpu.make_async_remote_copy(
            kv.at[a, g, held], kv.at[a, g, d],
            sem_kv_s.at[a, g, d], sem_kv_r.at[a, g, d], device_id=(along(d), tp), device_id_type=MESH)

    def ret_y(a, g, slot):
        return pltpu.make_async_remote_copy(
            ret_out.at[g, slot, a], ret_in.at[g, slot, a],
            sem_ret_s.at[a, g, slot], sem_ret_r.at[a, g, slot], device_id=(down, tp), device_id_type=MESH)

    def ret_x(a, g, d):
        return pltpu.make_async_remote_copy(
            ret_out.at[g, d, a], ret_in.at[g, d, a],
            sem_ret_s.at[a, g, d], sem_ret_r.at[a, g, d], device_id=(along(ROW - d), tp), device_id_type=MESH)

    def dq_local(g):
        return pltpu.make_async_copy(
            dq_stage.at[g, mine], dq_out.at[:, cols(tp * n_kv + g, wide)], sem_dq_l.at[g])

    def dq_remote(g):
        return pltpu.make_async_remote_copy(
            dq_stage.at[g, theirs], dq_out.at[:, cols(tp * n_kv + g, wide)],
            sem_dq_s.at[g], sem_dq_r.at[g], device_id=(ctx, other), device_id_type=MESH)

    dkvs = (dk_out, dv_out)

    def dkv_local(a, g):
        return pltpu.make_async_copy(
            dkv_stage.at[g, a, mine], dkvs[a].at[:, cols(tp * n_kv + g, HEAD_SIZE)], sem_dkv_l.at[a, g])

    def dkv_remote(a, g):
        return pltpu.make_async_remote_copy(
            dkv_stage.at[g, a, theirs], dkvs[a].at[:, cols(tp * n_kv + g, HEAD_SIZE)],
            sem_dkv_s.at[a, g], sem_dkv_r.at[a, g], device_id=(ctx, other), device_id_type=MESH)

    def start_remote(g):
        for a in (0, 1):
            narrow_remote(a, g).start()

    def forward_first(a, g):
        narrow_local(a, g).wait()
        narrow_remote(a, g).wait_recv()
        kv_y(a, g, 0).start()
        for d in (1, 3, 2):

            @pl.when(x + d < ROW)
            def _(d=d):
                kv_x(a, g, d).start()

    for g in range(n_kv):
        for a in (0, 1):
            narrow_local(a, g).start()
    for g in range(n_kv):
        for a in (0, 1, 2):
            wide_local(a, g).start()

    first = (ctx * SHARD).astype(F32)
    docs = len_ref.shape[1]
    lens = len_ref[...].astype(F32)
    r_d = lax.broadcasted_iota(jnp.int32, (docs, docs), 0)
    c_d = lax.broadcasted_iota(jnp.int32, (docs, docs), 1)
    starts = jnp.sum(jnp.where(c_d < r_d, jnp.broadcast_to(lens, (docs, docs)), 0.0), axis=1, keepdims=True)
    pos = lax.broadcasted_iota(jnp.int32, (docs, SHARD), 1).astype(F32) + first
    begin = jnp.max(jnp.where(starts <= pos, jnp.broadcast_to(starts, (docs, SHARD)), 0.0), axis=0, keepdims=True)
    begin = jnp.broadcast_to(begin, (SHARD, SHARD)).T
    q_row = lax.broadcasted_iota(jnp.int32, (SHARD, SHARD), 0).astype(F32) + first
    k_row = lax.broadcasted_iota(jnp.int32, (SHARD, SHARD), 1).astype(F32) + first

    def write_bias(s, carry):
        k_pos = k_row - (s * SHARD).astype(F32)
        keep = (k_pos >= begin) & (k_pos <= q_row)
        bias[s] = jnp.where(keep, 0.0, NEG)
        return carry

    lax.fori_loop(0, SLOTS, write_bias, 0)

    pl.semaphore_wait(barrier, 6)
    start_remote(0)
    wide_remote(0, 0).start()
    start_remote(1)
    forward_first(0, 0)
    forward_first(1, 0)
    for g in range(2, n_kv):
        start_remote(g)
    for g in range(n_kv):
        for a in (0, 1, 2):
            if (a, g) != (0, 0):
                wide_remote(a, g).start()
    forward_first(0, 1)
    forward_first(1, 1)

    def forward_x(a, g):
        kv_y(a, g, 0).wait_recv()
        for d in (1, 3, 2):

            @pl.when(x + d >= ROW)
            def _(d=d):
                kv_x(a, g, d).start()

    def forward_y(a, g, d):
        kv_x(a, g, d).wait_recv()
        kv_y(a, g, d).start()

    def back_x(g, d):
        par = lax.rem(g, 2)
        for a in (0, 1):
            ret_y(a, g, ROW + d).wait_recv()
            ret_out[g, d, a] = (acc[par, d, a] + ret_in[g, ROW + d, a].astype(F32)).astype(BF16)
            ret_x(a, g, d).start()

    def back_y(g):
        par = lax.rem(g, 2)
        for a in (0, 1):
            far = acc[par, ROW, a]
            near = acc[par, 0, a]
            for d in (1, 2, 3):
                ret_x(a, g, d).wait_recv()
                part = ret_in[g, d, a].astype(F32)
                crosses = ((x + d) // ROW).astype(F32)
                far = far + part * crosses
                near = near + part * (1.0 - crosses)
            ret_out[g, ROW, a] = far.astype(BF16)
            ret_y(a, g, ROW).start()
            acc[par, 0, a] = near

    def back_end(g):
        par = lax.rem(g, 2)
        for a in (0, 1):
            ret_y(a, g, ROW).wait_recv()
            total = acc[par, 0, a] + ret_in[g, ROW, a].astype(F32)
            dkv_stage[g, a] = total.T.astype(BF16)
            dkv_remote(a, g).start()
            dkv_local(a, g).start()

    def lanes(h, size):
        return pl.ds(pl.multiple_of(h * size, size), size)

    def head_cols(h):
        return slice(h * HEAD_SIZE, (h + 1) * HEAD_SIZE)

    def head_rows(h):
        return slice(h * SHARD, (h + 1) * SHARD)

    def twice(t):
        return jnp.concatenate([t, t], axis=1)

    sbufs = (sbuf0, sbuf1)
    topss = (tops0, tops1)

    def halves_max(sc):
        return jnp.maximum(sc[:, :HEAD_SIZE], sc[:, HEAD_SIZE:])

    def scores_step(g, s):
        keys_t = kv[0, g, s].T
        for h in range(width):
            tops = topss[h % 2]
            sc = dot_nn(qgo[0, g, :, head_cols(h)], keys_t)
            sc = sc * to_exp2 + bias[s]
            sbufs[h % 2][s, h // 2] = sc
            tops[h // 2] = jnp.maximum(tops[h // 2], halves_max(sc))

    def dq_head(g, h):
        left = jnp.concatenate([dsc[s, lanes(h, SHARD)] for s in range(SLOTS)], axis=1)
        right = kv[0, g].reshape(SLOTS * SHARD, HEAD_SIZE)
        dq_stage[g, :, lanes(h, HEAD_SIZE)] = (dot_nn(left, right) * inv_root).astype(BF16)

    def heads_step(g, new, old, before):
        if new is not None:
            h = 2 * new[0] + new[1]
            if before is not None:
                dq_head(before, h)
            q_new = qgo[0, g, :, lanes(h, HEAD_SIZE)]
            reach = None
        if old is not None:
            h = 2 * old[0] + old[1]
            sbuf = sbufs[old[1]]
            top = jnp.max(topss[old[1]][old[0]], axis=1, keepdims=True)
            total = jnp.zeros((SHARD, HEAD_SIZE), F32)
        for s in range(SLOTS):
            if old is not None:
                e = jnp.exp2(sbuf[s, old[0]] - top)
                sbuf[s, old[0]] = e
                total = total + (e[:, :HEAD_SIZE] + e[:, HEAD_SIZE:])
            if new is not None:
                sc = dot_nn(q_new, k_t[s]) * to_exp2 + bias[s]
                sbufs[new[1]][s, new[0]] = sc
                reach = halves_max(sc) if reach is None else jnp.maximum(reach, halves_max(sc))
        if new is not None:
            topss[new[1]][new[0]] = reach
        if old is not None:
            q_h = qgo[0, g, :, lanes(h, HEAD_SIZE)]
            g_h = qgo[1, g, :, lanes(h, HEAD_SIZE)]
            o_h = qgo[2, g, :, lanes(h, HEAD_SIZE)]
            q_t[:, lanes(h, SHARD)] = q_h.T
            g_t[:, lanes(h, SHARD)] = g_h.T
            delta = jnp.sum(g_h.astype(F32) * o_h.astype(F32), axis=1, keepdims=True)
            deltas[h] = jnp.broadcast_to(delta, (SHARD, HEAD_SIZE))
            total = jnp.sum(total, axis=1, keepdims=True)
            invs[h] = jnp.broadcast_to(1.0 / total, (SHARD, HEAD_SIZE))

    def grads_step(g, s):
        values_t = kv[1, g, s].T
        for h in range(width):
            g_h = qgo[1, g, :, head_cols(h)]
            p = sbufs[h % 2][s, h // 2] * twice(invs[h])
            dp = dot_nn(g_h, values_t)
            probs[head_rows(h)] = p.astype(BF16)
            dsc[s, head_rows(h)] = (p * (dp - twice(deltas[h]))).astype(BF16)
        dk = dot_nn(q_t[...], dsc[s]) * inv_root
        dv = dot_nn(g_t[...], probs[...])
        return dk, dv

    def send_dq(g):
        dq_remote(g).start()
        dq_local(g).start()

    def head_step(g, carry):
        par = lax.rem(g, 2)
        before = jnp.maximum(g - 1, 0)
        wide_local(0, g).wait()
        wide_remote(0, g).wait_recv()

        @pl.when(g > 1)
        def _():
            back_y(g - 2)

        @pl.when(g == 0)
        def _():
            tops0[...] = jnp.full(tops0.shape, 2 * NEG, F32)
            tops1[...] = jnp.full(tops1.shape, 2 * NEG, F32)

            def scores_of(i, carry_a):
                d = lax.select(i < 5, lax.select(i == 3, 3, lax.select(i == 4, 2, 1)),
                               lax.select(i == 6, 3, lax.select(i == 7, 2, 1)))
                s = lax.select(i == 0, 0, lax.select(i == 1, ROW, lax.select(i < 5, d, ROW + d)))

                @pl.when(i == 1)
                def _():
                    forward_x(0, g)

                @pl.when(i == 2)
                def _():
                    forward_x(1, g)

                @pl.when((i >= 2) & (i < 5))
                def _():
                    forward_y(0, g, d)

                @pl.when(i == 5)
                def _():
                    for e in (1, 3, 2):
                        forward_y(1, g, e)
                    for later in range(2, n_kv):
                        for a in (0, 1):
                            forward_first(a, later)
                    for a in (0, 1):
                        forward_x(a, 1)

                @pl.when(i >= 5)
                def _():
                    kv_y(0, g, d).wait_recv()

                scores_step(g, s)
                return carry_a

            lax.fori_loop(0, SLOTS, scores_of, 0)
            for a in (1, 2):
                wide_local(a, g).wait()
                wide_remote(a, g).wait_recv()

            def softmax_of(j, carry_s):
                heads_step(g, None, (j, 0), None)
                heads_step(g, None, (j, 1), None)
                return carry_s

            lax.fori_loop(0, width // 2, softmax_of, 0)

        @pl.when(g > 0)
        def _():
            for d in (1, 3, 2):
                kv_y(0, g, d).wait_recv()
            for a in (1, 2):
                wide_local(a, g).wait()
                wide_remote(a, g).wait_recv()
            for s in range(SLOTS):
                k_t[s] = kv[0, g, s].T
            heads_step(g, (0, 0), None, before)

            def heads_of(j, carry_s):
                heads_step(g, (j, 1), (j, 0), before)
                heads_step(g, (j + 1, 0), (j, 1), before)
                return carry_s

            lax.fori_loop(0, width // 2 - 1, heads_of, 0)
            tail = width // 2 - 1
            heads_step(g, (tail, 1), (tail, 0), before)
            heads_step(g, None, (tail, 1), None)
            send_dq(g - 1)

        def grads_of(i, carry_b):
            s = lax.select(i < 3, i + 5, lax.rem(i + 3, 5))

            @pl.when((g < n_kv - 1) & (i == 0))
            def _():
                for a in (0, 1):
                    for d in (1, 3, 2):
                        forward_y(a, g + 1, d)

            @pl.when((g < n_kv - 2) & (i == 4))
            def _():
                for a in (0, 1):
                    forward_x(a, g + 2)

            @pl.when((g > 0) & (i == 0))
            def _():
                for d in (1, 2, 3):
                    back_x(g - 1, d)

            @pl.when((g > 1) & (i == 0))
            def _():
                back_end(g - 2)

            @pl.when(i < 3)
            def _():
                kv_y(1, g, i + 1).wait_recv()

            dk, dv = grads_step(g, s)

            @pl.when(i < 3)
            def _():
                ret_out[g, s, 0] = dk.astype(BF16)
                ret_y(0, g, s).start()
                ret_out[g, s, 1] = dv.astype(BF16)
                ret_y(1, g, s).start()

            @pl.when(i >= 3)
            def _():
                acc[par, s, 0] = dk
                acc[par, s, 1] = dv

            return carry_b

        lax.fori_loop(0, SLOTS, grads_of, 0)
        return carry

    lax.fori_loop(0, n_kv, head_step, 0)
    last = jnp.int32(n_kv - 1)

    def last_dq(h, carry):
        dq_head(last, h)
        return carry

    def drain_early(g, carry):
        for a in (0, 1, 2):
            wide_remote(a, g).wait_send()
        for a in (0, 1):
            narrow_remote(a, g).wait_send()
            for d in range(ROW):
                kv_y(a, g, d).wait_send()
            for d in (1, 2, 3):
                kv_x(a, g, d).wait_send()
        return carry

    back_x(last, 1)
    lax.fori_loop(0, width // 2, last_dq, 0)
    back_y(last - 1)
    back_x(last, 2)
    lax.fori_loop(width // 2, width, last_dq, 0)
    back_x(last, 3)
    send_dq(last)
    back_end(last - 1)
    lax.fori_loop(0, n_kv, drain_early, 0)
    back_y(last)
    back_end(last)

    def drain(g, carry):
        for a in (0, 1):
            for s in range(ROW, SLOTS):
                ret_y(a, g, s).wait_send()
            for d in (1, 2, 3):
                ret_x(a, g, d).wait_send()
            dkv_local(a, g).wait()
            dkv_remote(a, g).wait()
        dq_local(g).wait()
        dq_remote(g).wait()
        return carry

    lax.fori_loop(0, n_kv, drain, 0)


def per_device(queries, key_matrix, value_matrix, attention_output, output_gradient, lengths):
    n_ctx = lax.axis_size("ctx")
    n_tp = lax.axis_size("tp")
    heads_q = queries.shape[1] // HEAD_SIZE
    heads_kv = key_matrix.shape[1] // HEAD_SIZE
    n_kv = heads_kv // n_tp
    width = heads_q // heads_kv
    wide = width * HEAD_SIZE
    dma = pltpu.SemaphoreType.DMA
    flops = 5 * 2 * SHARD * SLOTS * SHARD * HEAD_SIZE * n_kv * width
    raw = pl.pallas_call(
        functools.partial(kernel, n_ctx, n_kv, width),
        out_shape=(
            jax.ShapeDtypeStruct(queries.shape, BF16),
            jax.ShapeDtypeStruct(key_matrix.shape, BF16),
            jax.ShapeDtypeStruct(value_matrix.shape, BF16),
        ),
        in_specs=[pl.BlockSpec(memory_space=pl.ANY)] * 5 + [pl.BlockSpec(memory_space=pltpu.VMEM)],
        out_specs=(pl.BlockSpec(memory_space=pl.ANY),) * 3,
        scratch_shapes=[
            pltpu.VMEM((3, n_kv, SHARD, wide), BF16),
            pltpu.VMEM((2, n_kv, SLOTS, SHARD, HEAD_SIZE), BF16),
            pltpu.VMEM((SLOTS, width // 2, SHARD, SHARD), F32),
            pltpu.VMEM((SLOTS, width // 2, SHARD, SHARD), F32),
            pltpu.VMEM((SLOTS, SHARD, SHARD), F32),
            pltpu.VMEM((width // 2, SHARD, HEAD_SIZE), F32),
            pltpu.VMEM((width // 2, SHARD, HEAD_SIZE), F32),
            pltpu.VMEM((SLOTS, HEAD_SIZE, SHARD), BF16),
            pltpu.VMEM((width, SHARD, HEAD_SIZE), F32),
            pltpu.VMEM((width, SHARD, HEAD_SIZE), F32),
            pltpu.VMEM((HEAD_SIZE, width * SHARD), BF16),
            pltpu.VMEM((HEAD_SIZE, width * SHARD), BF16),
            pltpu.VMEM((width * SHARD, SHARD), BF16),
            pltpu.VMEM((SLOTS, width * SHARD, SHARD), BF16),
            pltpu.VMEM((2, ROW + 1, 2, HEAD_SIZE, SHARD), F32),
            pltpu.VMEM((n_kv, SLOTS, 2, HEAD_SIZE, SHARD), BF16),
            pltpu.VMEM((n_kv, SLOTS, 2, HEAD_SIZE, SHARD), BF16),
            pltpu.VMEM((n_kv, SHARD, wide), BF16),
            pltpu.VMEM((n_kv, 2, SHARD, HEAD_SIZE), BF16),
            dma((3, n_kv)),
            dma((3, n_kv)),
            dma((3, n_kv)),
            dma((2, n_kv)),
            dma((2, n_kv)),
            dma((2, n_kv)),
            dma((2, n_kv, SLOTS)),
            dma((2, n_kv, SLOTS)),
            dma((2, n_kv, SLOTS)),
            dma((2, n_kv, SLOTS)),
            dma((n_kv,)),
            dma((n_kv,)),
            dma((n_kv,)),
            dma((2, n_kv)),
            dma((2, n_kv)),
            dma((2, n_kv)),
        ],
        compiler_params=pltpu.CompilerParams(
            collective_id=0, has_side_effects=True, vmem_limit_bytes=62 * 1024 * 1024
        ),
        cost_estimate=pl.CostEstimate(
            flops=flops, bytes_accessed=10 * 1024 * 1024, transcendentals=flops // (10 * HEAD_SIZE)
        ),
        name="attention_backward",
    )(
        queries,
        key_matrix,
        value_matrix,
        attention_output,
        output_gradient,
        lengths.reshape(1, lengths.shape[0]),
    )
    return hand_over(*raw)


def hand_over_kernel(parts, dq_in, dk_in, dv_in, dq_out, dk_out, dv_out, dq_mid, dk_mid, dv_mid, sem_in, sem_out):
    rows = HALF // parts
    pieces = [(dk_in, dk_mid, dk_out), (dv_in, dv_mid, dv_out)]
    for i in range(parts):
        part = pl.ds(i * rows, rows)
        pieces.append((dq_in.at[part], dq_mid.at[part], dq_out.at[part]))
    loads = [pltpu.make_async_copy(a, b, sem_in.at[i]) for i, (a, b, _) in enumerate(pieces)]
    stores = [pltpu.make_async_copy(b, c, sem_out.at[i]) for i, (_, b, c) in enumerate(pieces)]
    for load in loads:
        load.start()
    for load, store in zip(loads, stores):
        load.wait()
        store.start()
    for store in stores:
        store.wait()


def hand_over(dq, dk, dv):
    parts = 8
    any_spec = pl.BlockSpec(memory_space=pl.ANY)
    arrays = (dq, dk, dv)
    return pl.pallas_call(
        functools.partial(hand_over_kernel, parts),
        out_shape=tuple(jax.ShapeDtypeStruct(t.shape, t.dtype) for t in arrays),
        in_specs=[any_spec] * 3,
        out_specs=(any_spec,) * 3,
        scratch_shapes=[pltpu.VMEM(t.shape, t.dtype) for t in arrays]
        + [pltpu.SemaphoreType.DMA((parts + 2,)), pltpu.SemaphoreType.DMA((parts + 2,))],
        name="hand_over",
    )(*arrays)


def solution(mesh):
    rows = P(("ctx", "tp"), None)
    return jax.shard_map(
        per_device,
        mesh=mesh,
        in_specs=(rows, rows, rows, rows, rows, P()),
        out_specs=(rows, rows, rows),
        check_vma=False,
    )
```

```python
import functools
import math

import jax
import jax.numpy as jnp
from jax import lax
from jax.experimental import pallas as pl
from jax.experimental.pallas import tpu as pltpu
from jax.sharding import PartitionSpec as P

HEAD_SIZE = 128
SHARD = 256
HALF = 128
SLOTS = 8
ROW = 4
NEG = -1e30
MESH = pl.DeviceIdType.MESH
F32 = jnp.float32
BF16 = jnp.bfloat16


def dot_nt(a, b):
    return lax.dot_general(a, b, (((1,), (1,)), ((), ())), preferred_element_type=F32)


def dot_nn(a, b):
    return jnp.dot(a, b, preferred_element_type=F32)


def kernel(
    n_ctx,
    n_kv,
    width,
    q_in,
    k_in,
    v_in,
    o_in,
    g_in,
    len_ref,
    dq_out,
    dk_out,
    dv_out,
    qgo,
    kv,
    sbuf0,
    sbuf1,
    bias,
    tops0,
    tops1,
    k_t,
    invs,
    deltas,
    q_t,
    g_t,
    probs,
    dsc,
    acc,
    ret_out,
    ret_in,
    dq_stage,
    dkv_stage,
    sem_qgo_l,
    sem_qgo_s,
    sem_qgo_r,
    sem_kv0_l,
    sem_kv0_s,
    sem_kv0_r,
    sem_kv_s,
    sem_kv_r,
    sem_ret_s,
    sem_ret_r,
    sem_dq_l,
    sem_dq_s,
    sem_dq_r,
    sem_dkv_l,
    sem_dkv_s,
    sem_dkv_r,
):
    ctx = lax.axis_index("ctx")
    tp = lax.axis_index("tp")
    x = lax.rem(ctx, ROW)
    row = ctx - x
    other = 1 - tp
    up = lax.rem(ctx + ROW, n_ctx)
    down = lax.rem(ctx + n_ctx - ROW, n_ctx)
    wide = width * HEAD_SIZE
    inv_root = HEAD_SIZE ** -0.5
    to_exp2 = inv_root * math.log2(math.e)

    def along(d):
        return row + lax.rem(x + d, ROW)

    barrier = pltpu.get_barrier_semaphore()
    for peer in [(ctx, other), (up, tp), (down, tp)] + [(along(d), tp) for d in (1, 2, 3)]:
        pl.semaphore_signal(barrier, inc=1, device_id=peer, device_id_type=MESH)
    def cols(head, size):
        return pl.ds(pl.multiple_of(head * size, size), size)

    mine = pl.ds(pl.multiple_of(tp * HALF, HALF), HALF)
    theirs = pl.ds(pl.multiple_of(other * HALF, HALF), HALF)
    wides = (q_in, g_in, o_in)
    narrows = (k_in, v_in)

    def wide_local(a, g):
        return pltpu.make_async_copy(
            wides[a].at[:, cols(tp * n_kv + g, wide)], qgo.at[a, g, mine], sem_qgo_l.at[a, g])

    def wide_remote(a, g):
        return pltpu.make_async_remote_copy(
            wides[a].at[:, cols(other * n_kv + g, wide)], qgo.at[a, g, mine],
            sem_qgo_s.at[a, g], sem_qgo_r.at[a, g], device_id=(ctx, other), device_id_type=MESH)

    def narrow_local(a, g):
        return pltpu.make_async_copy(
            narrows[a].at[:, cols(tp * n_kv + g, HEAD_SIZE)], kv.at[a, g, 0, mine], sem_kv0_l.at[a, g])

    def narrow_remote(a, g):
        return pltpu.make_async_remote_copy(
            narrows[a].at[:, cols(other * n_kv + g, HEAD_SIZE)], kv.at[a, g, 0, mine],
            sem_kv0_s.at[a, g], sem_kv0_r.at[a, g], device_id=(ctx, other), device_id_type=MESH)

    def kv_y(a, g, d):
        return pltpu.make_async_remote_copy(
            kv.at[a, g, d], kv.at[a, g, ROW + d],
            sem_kv_s.at[a, g, ROW + d], sem_kv_r.at[a, g, ROW + d], device_id=(up, tp), device_id_type=MESH)

    def kv_x(a, g, d):
        held = ROW * ((x + d) // ROW)
        return pltpu.make_async_remote_copy(
            kv.at[a, g, held], kv.at[a, g, d],
            sem_kv_s.at[a, g, d], sem_kv_r.at[a, g, d], device_id=(along(d), tp), device_id_type=MESH)

    def ret_y(a, g, slot):
        return pltpu.make_async_remote_copy(
            ret_out.at[g, slot, a], ret_in.at[g, slot, a],
            sem_ret_s.at[a, g, slot], sem_ret_r.at[a, g, slot], device_id=(down, tp), device_id_type=MESH)

    def ret_x(a, g, d):
        return pltpu.make_async_remote_copy(
            ret_out.at[g, d, a], ret_in.at[g, d, a],
            sem_ret_s.at[a, g, d], sem_ret_r.at[a, g, d], device_id=(along(ROW - d), tp), device_id_type=MESH)

    def dq_local(g):
        return pltpu.make_async_copy(
            dq_stage.at[g, mine], dq_out.at[:, cols(tp * n_kv + g, wide)], sem_dq_l.at[g])

    def dq_remote(g):
        return pltpu.make_async_remote_copy(
            dq_stage.at[g, theirs], dq_out.at[:, cols(tp * n_kv + g, wide)],
            sem_dq_s.at[g], sem_dq_r.at[g], device_id=(ctx, other), device_id_type=MESH)

    dkvs = (dk_out, dv_out)

    def dkv_local(a, g):
        return pltpu.make_async_copy(
            dkv_stage.at[g, a, mine], dkvs[a].at[:, cols(tp * n_kv + g, HEAD_SIZE)], sem_dkv_l.at[a, g])

    def dkv_remote(a, g):
        return pltpu.make_async_remote_copy(
            dkv_stage.at[g, a, theirs], dkvs[a].at[:, cols(tp * n_kv + g, HEAD_SIZE)],
            sem_dkv_s.at[a, g], sem_dkv_r.at[a, g], device_id=(ctx, other), device_id_type=MESH)

    def start_remote(g):
        for a in (0, 1):
            narrow_remote(a, g).start()

    def forward_first(a, g):
        narrow_local(a, g).wait()
        narrow_remote(a, g).wait_recv()
        kv_y(a, g, 0).start()

    for a in (0, 1):
        narrow_local(a, 0).start()
    wide_local(0, 0).start()

    pl.semaphore_wait(barrier, 6)
    start_remote(0)
    wide_remote(0, 0).start()
    start_remote(1)
    forward_first(0, 0)
    for d in (1, 3, 2):

        @pl.when(x + d < ROW)
        def _(d=d):
            kv_x(0, 0, d).start()

    forward_first(1, 0)
    for g in range(1, n_kv):
        for a in (0, 1):
            narrow_local(a, g).start()
        if g > 1:
            start_remote(g)
    for g in range(1, n_kv - 1):
        for a in (0, 1):
            forward_first(a, g)

    for g in range(n_kv):
        for a in (0, 1, 2):
            if (a, g) != (0, 0):
                wide_remote(a, g).start()
                wide_local(a, g).start()

    first = (ctx * SHARD).astype(F32)
    docs = len_ref.shape[1]
    lens = len_ref[...].astype(F32)
    r_d = lax.broadcasted_iota(jnp.int32, (docs, docs), 0)
    c_d = lax.broadcasted_iota(jnp.int32, (docs, docs), 1)
    starts = jnp.sum(jnp.where(c_d < r_d, jnp.broadcast_to(lens, (docs, docs)), 0.0), axis=1, keepdims=True)
    pos = lax.broadcasted_iota(jnp.int32, (docs, SHARD), 1).astype(F32) + first
    begin = jnp.max(jnp.where(starts <= pos, jnp.broadcast_to(starts, (docs, SHARD)), 0.0), axis=0, keepdims=True)
    begin = jnp.broadcast_to(begin, (SHARD, SHARD)).T
    q_row = lax.broadcasted_iota(jnp.int32, (SHARD, SHARD), 0).astype(F32) + first
    k_row = lax.broadcasted_iota(jnp.int32, (SHARD, SHARD), 1).astype(F32) + first

    def write_bias(s, carry):
        k_pos = k_row - (s * SHARD).astype(F32)
        keep = (k_pos >= begin) & (k_pos <= q_row)
        bias[s] = jnp.where(keep, 0.0, NEG)
        return carry

    lax.fori_loop(0, SLOTS, write_bias, 0)

    def forward_x(a, g):
        kv_y(a, g, 0).wait_recv()
        for d in (1, 3, 2):
            kv_x(a, g, d).start()

    def forward_y(a, g, d):
        kv_x(a, g, d).wait_recv()
        kv_y(a, g, d).start()

    def back_x(g, d):
        par = lax.rem(g, 2)
        for a in (0, 1):
            ret_y(a, g, ROW + d).wait_recv()
            ret_out[g, d, a] = (acc[par, d, a] + ret_in[g, ROW + d, a].astype(F32)).astype(BF16)
            ret_x(a, g, d).start()

    def back_y(g):
        par = lax.rem(g, 2)
        for a in (0, 1):
            far = acc[par, ROW, a]
            near = acc[par, 0, a]
            for d in (1, 2, 3):
                ret_x(a, g, d).wait_recv()
                part = ret_in[g, d, a].astype(F32)
                crosses = ((x + d) // ROW).astype(F32)
                far = far + part * crosses
                near = near + part * (1.0 - crosses)
            ret_out[g, ROW, a] = far.astype(BF16)
            ret_y(a, g, ROW).start()
            acc[par, 0, a] = near

    def back_end(g):
        par = lax.rem(g, 2)
        for a in (0, 1):
            ret_y(a, g, ROW).wait_recv()
            total = acc[par, 0, a] + ret_in[g, ROW, a].astype(F32)
            dkv_stage[g, a] = total.T.astype(BF16)
            dkv_remote(a, g).start()
            dkv_local(a, g).start()

    def lanes(h, size):
        return pl.ds(pl.multiple_of(h * size, size), size)

    def head_cols(h):
        return slice(h * HEAD_SIZE, (h + 1) * HEAD_SIZE)

    def head_rows(h):
        return slice(h * SHARD, (h + 1) * SHARD)

    def twice(t):
        return jnp.concatenate([t, t], axis=1)

    sbufs = (sbuf0, sbuf1)
    topss = (tops0, tops1)

    def halves_max(sc):
        return jnp.maximum(sc[:, :HEAD_SIZE], sc[:, HEAD_SIZE:])

    def scores_step(g, s):
        keys_t = kv[0, g, s].T
        for h in range(width):
            tops = topss[h % 2]
            sc = dot_nn(qgo[0, g, :, head_cols(h)], keys_t)
            sc = sc * to_exp2 + bias[s]
            sbufs[h % 2][s, h // 2] = sc
            tops[h // 2] = jnp.maximum(tops[h // 2], halves_max(sc))

    def dq_head(g, h):
        left = jnp.concatenate([dsc[s, lanes(h, SHARD)] for s in range(SLOTS)], axis=1)
        right = kv[0, g].reshape(SLOTS * SHARD, HEAD_SIZE)
        dq_stage[g, :, lanes(h, HEAD_SIZE)] = (dot_nn(left, right) * inv_root).astype(BF16)

    def exponentials(sbuf, hb, top, slots):
        total = jnp.zeros((SHARD, HEAD_SIZE), F32)
        for s in slots:
            e = jnp.exp2(sbuf[s, hb] - top)
            sbuf[s, hb] = e
            total = total + (e[:, :HEAD_SIZE] + e[:, HEAD_SIZE:])
        return total

    def turn_and_delta(g, h):
        q_h = qgo[0, g, :, lanes(h, HEAD_SIZE)]
        g_h = qgo[1, g, :, lanes(h, HEAD_SIZE)]
        o_h = qgo[2, g, :, lanes(h, HEAD_SIZE)]
        q_t[:, lanes(h, SHARD)] = q_h.T
        g_t[:, lanes(h, SHARD)] = g_h.T
        delta = jnp.sum(g_h.astype(F32) * o_h.astype(F32), axis=1, keepdims=True)
        deltas[h] = jnp.broadcast_to(delta, (SHARD, HEAD_SIZE))

    def near_softmax(j, carry):
        for par in (0, 1):
            h = 2 * j + par
            top = jnp.max(topss[par][j], axis=1, keepdims=True)
            invs[0, h] = jnp.broadcast_to(top, (SHARD, HEAD_SIZE))
            deltas[h] = exponentials(sbufs[par], j, top, range(ROW + 1))
        return carry

    def far_softmax(j, carry):
        for par in (0, 1):
            h = 2 * j + par
            top = jnp.max(topss[par][j], axis=1, keepdims=True)
            shrink = jnp.exp2(invs[0, h] - top)
            total = deltas[h] * shrink + exponentials(sbufs[par], j, top, range(ROW + 1, SLOTS))
            inv = jnp.broadcast_to(1.0 / jnp.sum(total, axis=1, keepdims=True), (SHARD, HEAD_SIZE))
            invs[1, h] = inv
            invs[0, h] = inv * shrink
            turn_and_delta(0, h)
        return carry

    def heads_step(g, new, old, before):
        if new is not None:
            h = 2 * new[0] + new[1]
            if before is not None:
                dq_head(before, h)
            q_new = qgo[0, g, :, lanes(h, HEAD_SIZE)]
            reach = None
        if old is not None:
            h = 2 * old[0] + old[1]
            sbuf = sbufs[old[1]]
            top = jnp.max(topss[old[1]][old[0]], axis=1, keepdims=True)
            total = jnp.zeros((SHARD, HEAD_SIZE), F32)
        for s in range(SLOTS):
            if old is not None:
                e = jnp.exp2(sbuf[s, old[0]] - top)
                sbuf[s, old[0]] = e
                total = total + (e[:, :HEAD_SIZE] + e[:, HEAD_SIZE:])
            if new is not None:
                sc = dot_nn(q_new, k_t[s]) * to_exp2 + bias[s]
                sbufs[new[1]][s, new[0]] = sc
                reach = halves_max(sc) if reach is None else jnp.maximum(reach, halves_max(sc))
        if new is not None:
            topss[new[1]][new[0]] = reach
        if old is not None:
            turn_and_delta(g, h)
            inv = jnp.broadcast_to(1.0 / jnp.sum(total, axis=1, keepdims=True), (SHARD, HEAD_SIZE))
            invs[1, h] = inv
            invs[0, h] = inv

    def grads_step(g, s):
        values_t = kv[1, g, s].T
        far = lax.select(s > ROW, 1, 0)
        for h in range(width):
            g_h = qgo[1, g, :, head_cols(h)]
            p = sbufs[h % 2][s, h // 2] * twice(invs[far, h])
            dp = dot_nn(g_h, values_t)
            probs[head_rows(h)] = p.astype(BF16)
            dsc[s, head_rows(h)] = (p * (dp - twice(deltas[h]))).astype(BF16)
        dk = dot_nn(q_t[...], dsc[s]) * inv_root
        dv = dot_nn(g_t[...], probs[...])
        return dk, dv

    def send_dq(g):
        dq_remote(g).start()
        dq_local(g).start()

    def head_step(g, carry):
        par = lax.rem(g, 2)
        before = jnp.maximum(g - 1, 0)
        wide_local(0, g).wait()
        wide_remote(0, g).wait_recv()

        @pl.when(g > 1)
        def _():
            back_y(g - 2)

        @pl.when(g == 0)
        def _():
            tops0[...] = jnp.full(tops0.shape, 2 * NEG, F32)
            tops1[...] = jnp.full(tops1.shape, 2 * NEG, F32)

            def scores_of(i, carry_a):
                d = lax.select(i < 5, lax.select(i == 3, 3, lax.select(i == 4, 2, 1)),
                               lax.select(i == 6, 3, lax.select(i == 7, 2, 1)))
                s = lax.select(i == 0, 0, lax.select(i == 1, ROW, lax.select(i < 5, d, ROW + d)))

                @pl.when(i == 1)
                def _():
                    kv_y(0, g, 0).wait_recv()
                    for e in (1, 3, 2):

                        @pl.when(x + e >= ROW)
                        def _(e=e):
                            kv_x(0, g, e).start()

                @pl.when(i == 2)
                def _():
                    forward_x(1, g)

                @pl.when((i >= 2) & (i < 5))
                def _():
                    forward_y(0, g, d)

                @pl.when(i == 5)
                def _():
                    for a in (0, 1):
                        forward_x(a, 1)
                    lax.fori_loop(0, width // 2, near_softmax, 0)
                    for e in (1, 3, 2):
                        forward_y(1, g, e)
                    for a in (0, 1):
                        forward_first(a, n_kv - 1)

                @pl.when(i >= 5)
                def _():
                    kv_y(0, g, d).wait_recv()

                scores_step(g, s)
                return carry_a

            lax.fori_loop(0, SLOTS, scores_of, 0)
            for a in (1, 2):
                wide_local(a, g).wait()
                wide_remote(a, g).wait_recv()

            lax.fori_loop(0, width // 2, far_softmax, 0)

        @pl.when(g > 0)
        def _():
            for d in (1, 3, 2):
                kv_y(0, g, d).wait_recv()
            for a in (1, 2):
                wide_local(a, g).wait()
                wide_remote(a, g).wait_recv()
            for s in range(SLOTS):
                k_t[s] = kv[0, g, s].T
            heads_step(g, (0, 0), None, before)

            def heads_of(j, carry_s):
                heads_step(g, (j, 1), (j, 0), before)
                heads_step(g, (j + 1, 0), (j, 1), before)
                return carry_s

            lax.fori_loop(0, width // 2 - 1, heads_of, 0)
            tail = width // 2 - 1
            heads_step(g, (tail, 1), (tail, 0), before)
            heads_step(g, None, (tail, 1), None)
            send_dq(g - 1)

        def grads_of(i, carry_b):
            s = lax.select(i < 3, i + 5, lax.rem(i + 3, 5))

            @pl.when((g < n_kv - 1) & (i == 0))
            def _():
                for a in (0, 1):
                    for d in (1, 3, 2):
                        forward_y(a, g + 1, d)

            @pl.when((g < n_kv - 2) & (i == 4))
            def _():
                for a in (0, 1):
                    forward_x(a, g + 2)

            @pl.when((g > 0) & (i == 0))
            def _():
                for d in (1, 2, 3):
                    back_x(g - 1, d)

            @pl.when((g > 1) & (i == 0))
            def _():
                back_end(g - 2)

            @pl.when(i < 3)
            def _():
                kv_y(1, g, i + 1).wait_recv()

            dk, dv = grads_step(g, s)

            @pl.when(i < 3)
            def _():
                ret_out[g, s, 0] = dk.astype(BF16)
                ret_y(0, g, s).start()
                ret_out[g, s, 1] = dv.astype(BF16)
                ret_y(1, g, s).start()

            @pl.when(i >= 3)
            def _():
                acc[par, s, 0] = dk
                acc[par, s, 1] = dv

            return carry_b

        lax.fori_loop(0, SLOTS, grads_of, 0)
        return carry

    lax.fori_loop(0, n_kv, head_step, 0)
    last = jnp.int32(n_kv - 1)

    def last_dq(h, carry):
        dq_head(last, h)
        return carry

    def drain_early(g, carry):
        for a in (0, 1, 2):
            wide_remote(a, g).wait_send()
        for a in (0, 1):
            narrow_remote(a, g).wait_send()
            for d in range(ROW):
                kv_y(a, g, d).wait_send()
            for d in (1, 2, 3):
                kv_x(a, g, d).wait_send()
        return carry

    back_x(last, 1)
    def drain(g, carry):
        for a in (0, 1):
            for s in range(ROW, SLOTS):
                ret_y(a, g, s).wait_send()
            for d in (1, 2, 3):
                ret_x(a, g, d).wait_send()
            dkv_local(a, g).wait()
            dkv_remote(a, g).wait()
        dq_local(g).wait()
        dq_remote(g).wait()
        return carry

    lax.fori_loop(0, width // 2, last_dq, 0)
    back_y(last - 1)
    back_x(last, 2)
    lax.fori_loop(width // 2, width, last_dq, 0)
    back_x(last, 3)
    send_dq(last)
    back_end(last - 1)
    lax.fori_loop(0, n_kv, drain_early, 0)
    back_y(last)
    lax.fori_loop(0, n_kv - 1, drain, 0)
    back_end(last)

    drain(last, 0)


def per_device(queries, key_matrix, value_matrix, attention_output, output_gradient, lengths):
    n_ctx = lax.axis_size("ctx")
    n_tp = lax.axis_size("tp")
    heads_q = queries.shape[1] // HEAD_SIZE
    heads_kv = key_matrix.shape[1] // HEAD_SIZE
    n_kv = heads_kv // n_tp
    width = heads_q // heads_kv
    wide = width * HEAD_SIZE
    dma = pltpu.SemaphoreType.DMA
    flops = 5 * 2 * SHARD * SLOTS * SHARD * HEAD_SIZE * n_kv * width
    raw = pl.pallas_call(
        functools.partial(kernel, n_ctx, n_kv, width),
        out_shape=(
            jax.ShapeDtypeStruct(queries.shape, BF16),
            jax.ShapeDtypeStruct(key_matrix.shape, BF16),
            jax.ShapeDtypeStruct(value_matrix.shape, BF16),
        ),
        in_specs=[pl.BlockSpec(memory_space=pl.ANY)] * 5 + [pl.BlockSpec(memory_space=pltpu.VMEM)],
        out_specs=(pl.BlockSpec(memory_space=pl.ANY),) * 3,
        scratch_shapes=[
            pltpu.VMEM((3, n_kv, SHARD, wide), BF16),
            pltpu.VMEM((2, n_kv, SLOTS, SHARD, HEAD_SIZE), BF16),
            pltpu.VMEM((SLOTS, width // 2, SHARD, SHARD), F32),
            pltpu.VMEM((SLOTS, width // 2, SHARD, SHARD), F32),
            pltpu.VMEM((SLOTS, SHARD, SHARD), F32),
            pltpu.VMEM((width // 2, SHARD, HEAD_SIZE), F32),
            pltpu.VMEM((width // 2, SHARD, HEAD_SIZE), F32),
            pltpu.VMEM((SLOTS, HEAD_SIZE, SHARD), BF16),
            pltpu.VMEM((2, width, SHARD, HEAD_SIZE), F32),
            pltpu.VMEM((width, SHARD, HEAD_SIZE), F32),
            pltpu.VMEM((HEAD_SIZE, width * SHARD), BF16),
            pltpu.VMEM((HEAD_SIZE, width * SHARD), BF16),
            pltpu.VMEM((width * SHARD, SHARD), BF16),
            pltpu.VMEM((SLOTS, width * SHARD, SHARD), BF16),
            pltpu.VMEM((2, ROW + 1, 2, HEAD_SIZE, SHARD), F32),
            pltpu.VMEM((n_kv, SLOTS, 2, HEAD_SIZE, SHARD), BF16),
            pltpu.VMEM((n_kv, SLOTS, 2, HEAD_SIZE, SHARD), BF16),
            pltpu.VMEM((n_kv, SHARD, wide), BF16),
            pltpu.VMEM((n_kv, 2, SHARD, HEAD_SIZE), BF16),
            dma((3, n_kv)),
            dma((3, n_kv)),
            dma((3, n_kv)),
            dma((2, n_kv)),
            dma((2, n_kv)),
            dma((2, n_kv)),
            dma((2, n_kv, SLOTS)),
            dma((2, n_kv, SLOTS)),
            dma((2, n_kv, SLOTS)),
            dma((2, n_kv, SLOTS)),
            dma((n_kv,)),
            dma((n_kv,)),
            dma((n_kv,)),
            dma((2, n_kv)),
            dma((2, n_kv)),
            dma((2, n_kv)),
        ],
        compiler_params=pltpu.CompilerParams(
            collective_id=0, has_side_effects=True, vmem_limit_bytes=62 * 1024 * 1024
        ),
        cost_estimate=pl.CostEstimate(
            flops=flops, bytes_accessed=10 * 1024 * 1024, transcendentals=flops // (10 * HEAD_SIZE)
        ),
        name="attention_backward",
    )(
        queries,
        key_matrix,
        value_matrix,
        attention_output,
        output_gradient,
        lengths.reshape(1, lengths.shape[0]),
    )
    return hand_over(*raw)


def hand_over_kernel(parts, dq_in, dk_in, dv_in, dq_out, dk_out, dv_out, dq_mid, dk_mid, dv_mid, sem_in, sem_out):
    rows = HALF // parts
    pieces = [(dk_in, dk_mid, dk_out), (dv_in, dv_mid, dv_out)]
    for i in range(parts):
        part = pl.ds(i * rows, rows)
        pieces.append((dq_in.at[part], dq_mid.at[part], dq_out.at[part]))
    loads = [pltpu.make_async_copy(a, b, sem_in.at[i]) for i, (a, b, _) in enumerate(pieces)]
    stores = [pltpu.make_async_copy(b, c, sem_out.at[i]) for i, (_, b, c) in enumerate(pieces)]
    for load in loads:
        load.start()
    for load, store in zip(loads, stores):
        load.wait()
        store.start()
    for store in stores:
        store.wait()


def hand_over(dq, dk, dv):
    parts = 8
    any_spec = pl.BlockSpec(memory_space=pl.ANY)
    arrays = (dq, dk, dv)
    return pl.pallas_call(
        functools.partial(hand_over_kernel, parts),
        out_shape=tuple(jax.ShapeDtypeStruct(t.shape, t.dtype) for t in arrays),
        in_specs=[any_spec] * 3,
        out_specs=(any_spec,) * 3,
        scratch_shapes=[pltpu.VMEM(t.shape, t.dtype) for t in arrays]
        + [pltpu.SemaphoreType.DMA((parts + 2,)), pltpu.SemaphoreType.DMA((parts + 2,))],
        name="hand_over",
    )(*arrays)


def solution(mesh):
    rows = P(("ctx", "tp"), None)
    return jax.shard_map(
        per_device,
        mesh=mesh,
        in_specs=(rows, rows, rows, rows, rows, P()),
        out_specs=(rows, rows, rows),
        check_vma=False,
    )
```

```python
import functools
import math

import jax
import jax.numpy as jnp
from jax import lax
from jax.experimental import pallas as pl
from jax.experimental.pallas import tpu as pltpu
from jax.sharding import PartitionSpec as P

HEAD_SIZE = 128
SHARD = 256
HALF = 128
SLOTS = 8
ROW = 4
NEG = -1e30
MESH = pl.DeviceIdType.MESH
F32 = jnp.float32
BF16 = jnp.bfloat16


def dot_nt(a, b):
    return lax.dot_general(a, b, (((1,), (1,)), ((), ())), preferred_element_type=F32)


def dot_nn(a, b):
    return jnp.dot(a, b, preferred_element_type=F32)


def kernel(
    n_ctx,
    n_kv,
    width,
    q_in,
    k_in,
    v_in,
    o_in,
    g_in,
    len_ref,
    dq_out,
    dk_out,
    dv_out,
    qgo,
    kv,
    sbuf0,
    sbuf1,
    bias,
    tops0,
    tops1,
    k_t,
    invs,
    deltas,
    q_t,
    g_t,
    probs,
    dsc,
    acc,
    ret_out,
    ret_in,
    dq_stage,
    dkv_stage,
    sem_qgo_l,
    sem_qgo_s,
    sem_qgo_r,
    sem_kv0_l,
    sem_kv0_s,
    sem_kv0_r,
    sem_kv_s,
    sem_kv_r,
    sem_ret_s,
    sem_ret_r,
    sem_dq_l,
    sem_dq_s,
    sem_dq_r,
    sem_dkv_l,
    sem_dkv_s,
    sem_dkv_r,
):
    ctx = lax.axis_index("ctx")
    tp = lax.axis_index("tp")
    x = lax.rem(ctx, ROW)
    row = ctx - x
    other = 1 - tp
    up = lax.rem(ctx + ROW, n_ctx)
    down = lax.rem(ctx + n_ctx - ROW, n_ctx)
    wide = width * HEAD_SIZE
    inv_root = HEAD_SIZE ** -0.5
    to_exp2 = inv_root * math.log2(math.e)

    def along(d):
        return row + lax.rem(x + d, ROW)

    barrier = pltpu.get_barrier_semaphore()
    for peer in [(ctx, other), (up, tp), (down, tp)] + [(along(d), tp) for d in (1, 2, 3)]:
        pl.semaphore_signal(barrier, inc=1, device_id=peer, device_id_type=MESH)
    def cols(head, size):
        return pl.ds(pl.multiple_of(head * size, size), size)

    mine = pl.ds(pl.multiple_of(tp * HALF, HALF), HALF)
    theirs = pl.ds(pl.multiple_of(other * HALF, HALF), HALF)
    wides = (q_in, g_in, o_in)
    narrows = (k_in, v_in)

    def wide_local(a, g):
        return pltpu.make_async_copy(
            wides[a].at[:, cols(tp * n_kv + g, wide)], qgo.at[a, g, mine], sem_qgo_l.at[a, g])

    def wide_remote(a, g):
        return pltpu.make_async_remote_copy(
            wides[a].at[:, cols(other * n_kv + g, wide)], qgo.at[a, g, mine],
            sem_qgo_s.at[a, g], sem_qgo_r.at[a, g], device_id=(ctx, other), device_id_type=MESH)

    def narrow_local(a, g):
        return pltpu.make_async_copy(
            narrows[a].at[:, cols(tp * n_kv + g, HEAD_SIZE)], kv.at[a, g, 0, mine], sem_kv0_l.at[a, g])

    def narrow_remote(a, g):
        return pltpu.make_async_remote_copy(
            narrows[a].at[:, cols(other * n_kv + g, HEAD_SIZE)], kv.at[a, g, 0, mine],
            sem_kv0_s.at[a, g], sem_kv0_r.at[a, g], device_id=(ctx, other), device_id_type=MESH)

    def kv_y(a, g, d):
        return pltpu.make_async_remote_copy(
            kv.at[a, g, d], kv.at[a, g, ROW + d],
            sem_kv_s.at[a, g, ROW + d], sem_kv_r.at[a, g, ROW + d], device_id=(up, tp), device_id_type=MESH)

    def kv_x(a, g, d):
        held = ROW * ((x + d) // ROW)
        return pltpu.make_async_remote_copy(
            kv.at[a, g, held], kv.at[a, g, d],
            sem_kv_s.at[a, g, d], sem_kv_r.at[a, g, d], device_id=(along(d), tp), device_id_type=MESH)

    def ret_y(a, g, slot):
        return pltpu.make_async_remote_copy(
            ret_out.at[g, slot - 1, a], ret_in.at[g, slot - 1, a],
            sem_ret_s.at[a, g, slot], sem_ret_r.at[a, g, slot], device_id=(down, tp), device_id_type=MESH)

    def ret_x(a, g, d):
        return pltpu.make_async_remote_copy(
            ret_out.at[g, d - 1, a], ret_in.at[g, d - 1, a],
            sem_ret_s.at[a, g, d], sem_ret_r.at[a, g, d], device_id=(along(ROW - d), tp), device_id_type=MESH)

    def dq_local(g):
        return pltpu.make_async_copy(
            dq_stage.at[lax.rem(g, 2), mine], dq_out.at[:, cols(tp * n_kv + g, wide)], sem_dq_l.at[g])

    def dq_remote(g):
        return pltpu.make_async_remote_copy(
            dq_stage.at[lax.rem(g, 2), theirs], dq_out.at[:, cols(tp * n_kv + g, wide)],
            sem_dq_s.at[g], sem_dq_r.at[g], device_id=(ctx, other), device_id_type=MESH)

    dkvs = (dk_out, dv_out)

    def dkv_local(a, g):
        return pltpu.make_async_copy(
            dkv_stage.at[g, a, mine], dkvs[a].at[:, cols(tp * n_kv + g, HEAD_SIZE)], sem_dkv_l.at[a, g])

    def dkv_remote(a, g):
        return pltpu.make_async_remote_copy(
            dkv_stage.at[g, a, theirs], dkvs[a].at[:, cols(tp * n_kv + g, HEAD_SIZE)],
            sem_dkv_s.at[a, g], sem_dkv_r.at[a, g], device_id=(ctx, other), device_id_type=MESH)

    def start_remote(g):
        for a in (0, 1):
            narrow_remote(a, g).start()

    def forward_first(a, g):
        narrow_local(a, g).wait()
        narrow_remote(a, g).wait_recv()
        kv_y(a, g, 0).start()

    for a in (0, 1):
        narrow_local(a, 0).start()
    wide_local(0, 0).start()

    pl.semaphore_wait(barrier, 6)
    start_remote(0)
    wide_remote(0, 0).start()
    start_remote(1)
    forward_first(0, 0)
    for d in (1, 3, 2):

        @pl.when(x + d < ROW)
        def _(d=d):
            kv_x(0, 0, d).start()

    forward_first(1, 0)
    for g in range(1, n_kv):
        for a in (0, 1):
            narrow_local(a, g).start()
        if g > 1:
            start_remote(g)
    for g in range(1, n_kv - 1):
        for a in (0, 1):
            forward_first(a, g)

    for g in range(n_kv):
        for a in (0, 1, 2):
            if (a, g) != (0, 0):
                wide_remote(a, g).start()
                wide_local(a, g).start()

    first = (ctx * SHARD).astype(F32)
    docs = len_ref.shape[1]
    lens = len_ref[...].astype(F32)
    r_d = lax.broadcasted_iota(jnp.int32, (docs, docs), 0)
    c_d = lax.broadcasted_iota(jnp.int32, (docs, docs), 1)
    starts = jnp.sum(jnp.where(c_d < r_d, jnp.broadcast_to(lens, (docs, docs)), 0.0), axis=1, keepdims=True)
    pos = lax.broadcasted_iota(jnp.int32, (docs, SHARD), 1).astype(F32) + first
    begin = jnp.max(jnp.where(starts <= pos, jnp.broadcast_to(starts, (docs, SHARD)), 0.0), axis=0, keepdims=True)
    begin = jnp.broadcast_to(begin, (SHARD, SHARD)).T
    q_row = lax.broadcasted_iota(jnp.int32, (SHARD, SHARD), 0).astype(F32) + first
    k_row = lax.broadcasted_iota(jnp.int32, (SHARD, SHARD), 1).astype(F32) + first

    def write_bias(s, carry):
        k_pos = k_row - (s * SHARD).astype(F32)
        keep = (k_pos >= begin) & (k_pos <= q_row)
        bias[s] = jnp.where(keep, 0.0, NEG)
        return carry

    lax.fori_loop(0, SLOTS, write_bias, 0)

    def forward_x(a, g):
        kv_y(a, g, 0).wait_recv()
        for d in (1, 3, 2):
            kv_x(a, g, d).start()

    def forward_y(a, g, d):
        kv_x(a, g, d).wait_recv()
        kv_y(a, g, d).start()

    def back_x(g, d):
        par = lax.rem(g, 2)
        for a in (0, 1):
            ret_y(a, g, ROW + d).wait_recv()
            ret_out[g, d - 1, a] = (acc[par, d, a] + ret_in[g, ROW + d - 1, a].astype(F32)).astype(BF16)
            ret_x(a, g, d).start()

    def back_y(g):
        par = lax.rem(g, 2)
        for a in (0, 1):
            far = acc[par, ROW, a]
            near = acc[par, 0, a]
            for d in (1, 2, 3):
                ret_x(a, g, d).wait_recv()
                part = ret_in[g, d - 1, a].astype(F32)
                crosses = ((x + d) // ROW).astype(F32)
                far = far + part * crosses
                near = near + part * (1.0 - crosses)
            ret_out[g, ROW - 1, a] = far.astype(BF16)
            ret_y(a, g, ROW).start()
            acc[par, 0, a] = near

    def back_end(g):
        par = lax.rem(g, 2)
        for a in (0, 1):
            ret_y(a, g, ROW).wait_recv()
            total = acc[par, 0, a] + ret_in[g, ROW - 1, a].astype(F32)
            dkv_stage[g, a] = total.T.astype(BF16)
            dkv_remote(a, g).start()
            dkv_local(a, g).start()

    def lanes(h, size):
        return pl.ds(pl.multiple_of(h * size, size), size)

    def head_cols(h):
        return slice(h * HEAD_SIZE, (h + 1) * HEAD_SIZE)

    def head_rows(h):
        return slice(h * SHARD, (h + 1) * SHARD)

    def twice(t):
        return jnp.concatenate([t, t], axis=1)

    sbufs = (sbuf0, sbuf1)
    topss = (tops0, tops1)

    def halves_max(sc):
        return jnp.maximum(sc[:, :HEAD_SIZE], sc[:, HEAD_SIZE:])

    def scores_step(g, s):
        keys_t = kv[0, g, s].T
        for h in range(width):
            tops = topss[h % 2]
            sc = dot_nn(qgo[0, g, :, head_cols(h)], keys_t)
            sc = sc * to_exp2 + bias[s]
            sbufs[h % 2][s, h // 2] = sc
            tops[h // 2] = jnp.maximum(tops[h // 2], halves_max(sc))

    def dq_head(g, h):
        par = lax.rem(g, 2)
        left = jnp.concatenate([dsc[par, s, lanes(h, SHARD)] for s in range(SLOTS)], axis=1)
        right = kv[0, g].reshape(SLOTS * SHARD, HEAD_SIZE)
        dq_stage[par, :, lanes(h, HEAD_SIZE)] = (dot_nn(left, right) * inv_root).astype(BF16)

    def exponentials(sbuf, hb, top, slots):
        total = jnp.zeros((SHARD, HEAD_SIZE), F32)
        for s in slots:
            e = jnp.exp2(sbuf[s, hb] - top)
            sbuf[s, hb] = e
            total = total + (e[:, :HEAD_SIZE] + e[:, HEAD_SIZE:])
        return total

    def turn_and_delta(g, h):
        q_h = qgo[0, g, :, lanes(h, HEAD_SIZE)]
        g_h = qgo[1, g, :, lanes(h, HEAD_SIZE)]
        o_h = qgo[2, g, :, lanes(h, HEAD_SIZE)]
        q_t[:, lanes(h, SHARD)] = q_h.T
        g_t[:, lanes(h, SHARD)] = g_h.T
        delta = jnp.sum(g_h.astype(F32) * o_h.astype(F32), axis=1, keepdims=True)
        deltas[h] = jnp.broadcast_to(delta, (SHARD, HEAD_SIZE))

    def near_softmax(j, carry):
        for par in (0, 1):
            h = 2 * j + par
            top = jnp.max(topss[par][j], axis=1, keepdims=True)
            invs[0, h] = jnp.broadcast_to(top, (SHARD, HEAD_SIZE))
            deltas[h] = exponentials(sbufs[par], j, top, range(ROW + 1))
        return carry

    def far_softmax(j, carry):
        for par in (0, 1):
            h = 2 * j + par
            top = jnp.max(topss[par][j], axis=1, keepdims=True)
            shrink = jnp.exp2(invs[0, h] - top)
            total = deltas[h] * shrink + exponentials(sbufs[par], j, top, range(ROW + 1, SLOTS))
            inv = jnp.broadcast_to(1.0 / jnp.sum(total, axis=1, keepdims=True), (SHARD, HEAD_SIZE))
            invs[1, h] = inv
            invs[0, h] = inv * shrink
            turn_and_delta(0, h)
        return carry

    def heads_step(g, new, old, before):
        if new is not None:
            h = 2 * new[0] + new[1]
            if before is not None:
                dq_head(before, h)
            q_new = qgo[0, g, :, lanes(h, HEAD_SIZE)]
            reach = None
        if old is not None:
            h = 2 * old[0] + old[1]
            sbuf = sbufs[old[1]]
            top = jnp.max(topss[old[1]][old[0]], axis=1, keepdims=True)
            total = jnp.zeros((SHARD, HEAD_SIZE), F32)
        for s in range(SLOTS):
            if old is not None:
                e = jnp.exp2(sbuf[s, old[0]] - top)
                sbuf[s, old[0]] = e
                total = total + (e[:, :HEAD_SIZE] + e[:, HEAD_SIZE:])
            if new is not None:
                sc = dot_nn(q_new, k_t[s]) * to_exp2 + bias[s]
                sbufs[new[1]][s, new[0]] = sc
                reach = halves_max(sc) if reach is None else jnp.maximum(reach, halves_max(sc))
        if new is not None:
            topss[new[1]][new[0]] = reach
        if old is not None:
            turn_and_delta(g, h)
            inv = jnp.broadcast_to(1.0 / jnp.sum(total, axis=1, keepdims=True), (SHARD, HEAD_SIZE))
            invs[1, h] = inv
            invs[0, h] = inv

    def grads_step(g, s):
        values_t = kv[1, g, s].T
        par = lax.rem(g, 2)
        far = lax.select(s > ROW, 1, 0)
        for h in range(width):
            g_h = qgo[1, g, :, head_cols(h)]
            p = sbufs[h % 2][s, h // 2] * twice(invs[far, h])
            dp = dot_nn(g_h, values_t)
            probs[head_rows(h)] = p.astype(BF16)
            dsc[par, s, head_rows(h)] = (p * (dp - twice(deltas[h]))).astype(BF16)
        dk = dot_nn(q_t[...], dsc[par, s]) * inv_root
        dv = dot_nn(g_t[...], probs[...])
        return dk, dv

    def send_dq(g):
        dq_remote(g).start()
        dq_local(g).start()

    def head_step(g, carry):
        par = lax.rem(g, 2)
        wide_local(0, g).wait()
        wide_remote(0, g).wait_recv()

        @pl.when(g > 1)
        def _():
            back_y(g - 2)

        @pl.when(g == 0)
        def _():
            tops0[...] = jnp.full(tops0.shape, 2 * NEG, F32)
            tops1[...] = jnp.full(tops1.shape, 2 * NEG, F32)

            def scores_of(i, carry_a):
                d = lax.select(i < 5, lax.select(i == 3, 3, lax.select(i == 4, 2, 1)),
                               lax.select(i == 6, 3, lax.select(i == 7, 2, 1)))
                s = lax.select(i == 0, 0, lax.select(i == 1, ROW, lax.select(i < 5, d, ROW + d)))

                @pl.when(i == 1)
                def _():
                    kv_y(0, g, 0).wait_recv()
                    for e in (1, 3, 2):

                        @pl.when(x + e >= ROW)
                        def _(e=e):
                            kv_x(0, g, e).start()

                @pl.when(i == 2)
                def _():
                    forward_x(1, g)

                @pl.when((i >= 2) & (i < 5))
                def _():
                    forward_y(0, g, d)

                @pl.when(i == 5)
                def _():
                    for a in (0, 1):
                        forward_x(a, 1)
                    lax.fori_loop(0, width // 2, near_softmax, 0)
                    for e in (1, 3, 2):
                        forward_y(1, g, e)
                    for a in (0, 1):
                        forward_first(a, n_kv - 1)

                @pl.when(i >= 5)
                def _():
                    kv_y(0, g, d).wait_recv()

                scores_step(g, s)
                return carry_a

            lax.fori_loop(0, SLOTS, scores_of, 0)
            for a in (1, 2):
                wide_local(a, g).wait()
                wide_remote(a, g).wait_recv()

            lax.fori_loop(0, width // 2, far_softmax, 0)

        def later_group(before):
            for d in (1, 3, 2):
                kv_y(0, g, d).wait_recv()
            for a in (1, 2):
                wide_local(a, g).wait()
                wide_remote(a, g).wait_recv()
            for s in range(SLOTS):
                k_t[s] = kv[0, g, s].T
            heads_step(g, (0, 0), None, before)

            def heads_of(j, carry_s):
                heads_step(g, (j, 1), (j, 0), before)
                heads_step(g, (j + 1, 0), (j, 1), before)
                return carry_s

            lax.fori_loop(0, width // 2 - 1, heads_of, 0)
            tail = width // 2 - 1
            heads_step(g, (tail, 1), (tail, 0), before)
            heads_step(g, None, (tail, 1), None)

        @pl.when((g > 0) & (g < n_kv - 1))
        def _():
            later_group(g - 1)
            send_dq(g - 1)

        @pl.when(g == n_kv - 1)
        def _():
            later_group(None)

        def grads_of(i, carry_b):
            s = lax.select(i < 3, i + 5, lax.rem(i + 3, 5))

            @pl.when((g < n_kv - 1) & (i == 0))
            def _():
                for a in (0, 1):
                    for d in (1, 3, 2):
                        forward_y(a, g + 1, d)

            @pl.when((g < n_kv - 2) & (i == 4))
            def _():
                for a in (0, 1):
                    forward_x(a, g + 2)

            @pl.when((g > 0) & (i == 0))
            def _():
                for d in (1, 2, 3):
                    back_x(g - 1, d)

            @pl.when((g > 1) & (i == 0))
            def _():
                back_end(g - 2)

            @pl.when(i < 3)
            def _():
                kv_y(1, g, i + 1).wait_recv()

            dk, dv = grads_step(g, s)

            @pl.when(i < 3)
            def _():
                ret_out[g, s - 1, 0] = dk.astype(BF16)
                ret_y(0, g, s).start()
                ret_out[g, s - 1, 1] = dv.astype(BF16)
                ret_y(1, g, s).start()

            @pl.when(i >= 3)
            def _():
                acc[par, s, 0] = dk
                acc[par, s, 1] = dv

            return carry_b

        lax.fori_loop(0, SLOTS, grads_of, 0)
        return carry

    lax.fori_loop(0, n_kv, head_step, 0)
    last = jnp.int32(n_kv - 1)

    def last_dq(i, carry):
        dq_head(last - 1 + i // width, lax.rem(i, width))
        return carry

    def drain_early(g, carry):
        for a in (0, 1, 2):
            wide_remote(a, g).wait_send()
        for a in (0, 1):
            narrow_remote(a, g).wait_send()
            for d in range(ROW):
                kv_y(a, g, d).wait_send()
            for d in (1, 2, 3):
                kv_x(a, g, d).wait_send()
        return carry

    back_x(last, 1)
    def drain(g, carry):
        for a in (0, 1):
            for s in range(ROW, SLOTS):
                ret_y(a, g, s).wait_send()
            for d in (1, 2, 3):
                ret_x(a, g, d).wait_send()
            dkv_local(a, g).wait()
            dkv_remote(a, g).wait()
        return carry

    for g in range(n_kv - 2):
        dq_local(g).wait()
        dq_remote(g).wait_send()
    half = width // 2
    lax.fori_loop(0, half, last_dq, 0)
    back_y(last - 1)
    back_x(last, 2)
    lax.fori_loop(half, 3 * half, last_dq, 0)
    back_x(last, 3)
    send_dq(last - 1)
    lax.fori_loop(3 * half, 4 * half, last_dq, 0)
    send_dq(last)
    back_end(last - 1)
    lax.fori_loop(0, n_kv, drain_early, 0)
    back_y(last)
    lax.fori_loop(0, n_kv - 1, drain, 0)
    back_end(last)

    drain(last, 0)
    for g in range(n_kv):
        if g >= n_kv - 2:
            dq_local(g).wait()
            dq_remote(g).wait_send()
        dq_remote(g).wait_recv()


def per_device(queries, key_matrix, value_matrix, attention_output, output_gradient, lengths):
    n_ctx = lax.axis_size("ctx")
    n_tp = lax.axis_size("tp")
    heads_q = queries.shape[1] // HEAD_SIZE
    heads_kv = key_matrix.shape[1] // HEAD_SIZE
    n_kv = heads_kv // n_tp
    width = heads_q // heads_kv
    wide = width * HEAD_SIZE
    dma = pltpu.SemaphoreType.DMA
    flops = 5 * 2 * SHARD * SLOTS * SHARD * HEAD_SIZE * n_kv * width
    raw = pl.pallas_call(
        functools.partial(kernel, n_ctx, n_kv, width),
        out_shape=(
            jax.ShapeDtypeStruct(queries.shape, BF16),
            jax.ShapeDtypeStruct(key_matrix.shape, BF16),
            jax.ShapeDtypeStruct(value_matrix.shape, BF16),
        ),
        in_specs=[pl.BlockSpec(memory_space=pl.ANY)] * 5 + [pl.BlockSpec(memory_space=pltpu.VMEM)],
        out_specs=(pl.BlockSpec(memory_space=pl.ANY),) * 3,
        scratch_shapes=[
            pltpu.VMEM((3, n_kv, SHARD, wide), BF16),
            pltpu.VMEM((2, n_kv, SLOTS, SHARD, HEAD_SIZE), BF16),
            pltpu.VMEM((SLOTS, width // 2, SHARD, SHARD), F32),
            pltpu.VMEM((SLOTS, width // 2, SHARD, SHARD), F32),
            pltpu.VMEM((SLOTS, SHARD, SHARD), F32),
            pltpu.VMEM((width // 2, SHARD, HEAD_SIZE), F32),
            pltpu.VMEM((width // 2, SHARD, HEAD_SIZE), F32),
            pltpu.VMEM((SLOTS, HEAD_SIZE, SHARD), BF16),
            pltpu.VMEM((2, width, SHARD, HEAD_SIZE), F32),
            pltpu.VMEM((width, SHARD, HEAD_SIZE), F32),
            pltpu.VMEM((HEAD_SIZE, width * SHARD), BF16),
            pltpu.VMEM((HEAD_SIZE, width * SHARD), BF16),
            pltpu.VMEM((width * SHARD, SHARD), BF16),
            pltpu.VMEM((2, SLOTS, width * SHARD, SHARD), BF16),
            pltpu.VMEM((2, ROW + 1, 2, HEAD_SIZE, SHARD), F32),
            pltpu.VMEM((n_kv, SLOTS - 1, 2, HEAD_SIZE, SHARD), BF16),
            pltpu.VMEM((n_kv, SLOTS - 1, 2, HEAD_SIZE, SHARD), BF16),
            pltpu.VMEM((2, SHARD, wide), BF16),
            pltpu.VMEM((n_kv, 2, SHARD, HEAD_SIZE), BF16),
            dma((3, n_kv)),
            dma((3, n_kv)),
            dma((3, n_kv)),
            dma((2, n_kv)),
            dma((2, n_kv)),
            dma((2, n_kv)),
            dma((2, n_kv, SLOTS)),
            dma((2, n_kv, SLOTS)),
            dma((2, n_kv, SLOTS)),
            dma((2, n_kv, SLOTS)),
            dma((n_kv,)),
            dma((n_kv,)),
            dma((n_kv,)),
            dma((2, n_kv)),
            dma((2, n_kv)),
            dma((2, n_kv)),
        ],
        compiler_params=pltpu.CompilerParams(
            collective_id=0, has_side_effects=True, vmem_limit_bytes=64 * 1024 * 1024 - 65536
        ),
        cost_estimate=pl.CostEstimate(
            flops=flops, bytes_accessed=10 * 1024 * 1024, transcendentals=flops // (10 * HEAD_SIZE)
        ),
        name="attention_backward",
    )(
        queries,
        key_matrix,
        value_matrix,
        attention_output,
        output_gradient,
        lengths.reshape(1, lengths.shape[0]),
    )
    return hand_over(*raw)


def hand_over_kernel(parts, dq_in, dk_in, dv_in, dq_out, dk_out, dv_out, dq_mid, dk_mid, dv_mid, sem_in, sem_out):
    rows = HALF // parts
    pieces = [(dk_in, dk_mid, dk_out), (dv_in, dv_mid, dv_out)]
    for i in range(parts):
        part = pl.ds(i * rows, rows)
        pieces.append((dq_in.at[part], dq_mid.at[part], dq_out.at[part]))
    loads = [pltpu.make_async_copy(a, b, sem_in.at[i]) for i, (a, b, _) in enumerate(pieces)]
    stores = [pltpu.make_async_copy(b, c, sem_out.at[i]) for i, (_, b, c) in enumerate(pieces)]
    for load in loads:
        load.start()
    for load, store in zip(loads, stores):
        load.wait()
        store.start()
    for store in stores:
        store.wait()


def hand_over(dq, dk, dv):
    parts = 8
    any_spec = pl.BlockSpec(memory_space=pl.ANY)
    arrays = (dq, dk, dv)
    return pl.pallas_call(
        functools.partial(hand_over_kernel, parts),
        out_shape=tuple(jax.ShapeDtypeStruct(t.shape, t.dtype) for t in arrays),
        in_specs=[any_spec] * 3,
        out_specs=(any_spec,) * 3,
        scratch_shapes=[pltpu.VMEM(t.shape, t.dtype) for t in arrays]
        + [pltpu.SemaphoreType.DMA((parts + 2,)), pltpu.SemaphoreType.DMA((parts + 2,))],
        name="hand_over",
    )(*arrays)


def solution(mesh):
    rows = P(("ctx", "tp"), None)
    return jax.shard_map(
        per_device,
        mesh=mesh,
        in_specs=(rows, rows, rows, rows, rows, P()),
        out_specs=(rows, rows, rows),
        check_vma=False,
    )
```

```python
import functools
import math

import jax
import jax.numpy as jnp
from jax import lax
from jax.experimental import pallas as pl
from jax.experimental.pallas import tpu as pltpu
from jax.sharding import PartitionSpec as P

HEAD_SIZE = 128
SHARD = 256
HALF = 128
SLOTS = 8
ROW = 4
NEG = -1e30
MESH = pl.DeviceIdType.MESH
F32 = jnp.float32
BF16 = jnp.bfloat16


def dot_nt(a, b):
    return lax.dot_general(a, b, (((1,), (1,)), ((), ())), preferred_element_type=F32)


def dot_nn(a, b):
    return jnp.dot(a, b, preferred_element_type=F32)


def kernel(
    n_ctx,
    n_kv,
    width,
    q_in,
    k_in,
    v_in,
    o_in,
    g_in,
    len_ref,
    dq_out,
    dk_out,
    dv_out,
    qgo,
    kv,
    sbuf0,
    sbuf1,
    bias,
    tops0,
    tops1,
    k_t,
    invs,
    deltas,
    q_t,
    g_t,
    probs,
    dsc,
    acc,
    ret_out,
    ret_in,
    dq_stage,
    dkv_stage,
    sem_qgo_l,
    sem_qgo_s,
    sem_qgo_r,
    sem_kv0_l,
    sem_kv0_s,
    sem_kv0_r,
    sem_kv_s,
    sem_kv_r,
    sem_ret_s,
    sem_ret_r,
    sem_dq_l,
    sem_dq_s,
    sem_dq_r,
    sem_dkv_l,
    sem_dkv_s,
    sem_dkv_r,
):
    ctx = lax.axis_index("ctx")
    tp = lax.axis_index("tp")
    x = lax.rem(ctx, ROW)
    row = ctx - x
    other = 1 - tp
    up = lax.rem(ctx + ROW, n_ctx)
    down = lax.rem(ctx + n_ctx - ROW, n_ctx)
    wide = width * HEAD_SIZE
    inv_root = HEAD_SIZE ** -0.5
    to_exp2 = inv_root * math.log2(math.e)

    def along(d):
        return row + lax.rem(x + d, ROW)

    barrier = pltpu.get_barrier_semaphore()
    for peer in [(ctx, other), (up, tp), (down, tp)] + [(along(d), tp) for d in (1, 2, 3)]:
        pl.semaphore_signal(barrier, inc=1, device_id=peer, device_id_type=MESH)
    def cols(head, size):
        return pl.ds(pl.multiple_of(head * size, size), size)

    mine = pl.ds(pl.multiple_of(tp * HALF, HALF), HALF)
    theirs = pl.ds(pl.multiple_of(other * HALF, HALF), HALF)
    wides = (q_in, g_in, o_in)
    narrows = (k_in, v_in)

    def wide_local(a, g):
        return pltpu.make_async_copy(
            wides[a].at[:, cols(tp * n_kv + g, wide)], qgo.at[a, g, mine], sem_qgo_l.at[a, g])

    def wide_remote(a, g):
        return pltpu.make_async_remote_copy(
            wides[a].at[:, cols(other * n_kv + g, wide)], qgo.at[a, g, mine],
            sem_qgo_s.at[a, g], sem_qgo_r.at[a, g], device_id=(ctx, other), device_id_type=MESH)

    def narrow_local(a, g):
        return pltpu.make_async_copy(
            narrows[a].at[:, cols(tp * n_kv + g, HEAD_SIZE)], kv.at[a, g, 0, mine], sem_kv0_l.at[a, g])

    def narrow_remote(a, g):
        return pltpu.make_async_remote_copy(
            narrows[a].at[:, cols(other * n_kv + g, HEAD_SIZE)], kv.at[a, g, 0, mine],
            sem_kv0_s.at[a, g], sem_kv0_r.at[a, g], device_id=(ctx, other), device_id_type=MESH)

    def kv_y(a, g, d):
        return pltpu.make_async_remote_copy(
            kv.at[a, g, d], kv.at[a, g, ROW + d],
            sem_kv_s.at[a, g, ROW + d], sem_kv_r.at[a, g, ROW + d], device_id=(up, tp), device_id_type=MESH)

    def kv_x(a, g, d):
        held = ROW * ((x + d) // ROW)
        return pltpu.make_async_remote_copy(
            kv.at[a, g, held], kv.at[a, g, d],
            sem_kv_s.at[a, g, d], sem_kv_r.at[a, g, d], device_id=(along(d), tp), device_id_type=MESH)

    def ret_y(a, g, slot):
        return pltpu.make_async_remote_copy(
            ret_out.at[g, slot - 1, a], ret_in.at[g, slot - 1, a],
            sem_ret_s.at[a, g, slot], sem_ret_r.at[a, g, slot], device_id=(down, tp), device_id_type=MESH)

    def ret_x(a, g, d):
        return pltpu.make_async_remote_copy(
            ret_out.at[g, d - 1, a], ret_in.at[g, d - 1, a],
            sem_ret_s.at[a, g, d], sem_ret_r.at[a, g, d], device_id=(along(ROW - d), tp), device_id_type=MESH)

    def dq_local(g):
        return pltpu.make_async_copy(
            dq_stage.at[lax.rem(g, 2), mine], dq_out.at[:, cols(tp * n_kv + g, wide)], sem_dq_l.at[g])

    def dq_remote(g):
        return pltpu.make_async_remote_copy(
            dq_stage.at[lax.rem(g, 2), theirs], dq_out.at[:, cols(tp * n_kv + g, wide)],
            sem_dq_s.at[g], sem_dq_r.at[g], device_id=(ctx, other), device_id_type=MESH)

    dkvs = (dk_out, dv_out)

    def dkv_local(a, g):
        return pltpu.make_async_copy(
            dkv_stage.at[g, a, mine], dkvs[a].at[:, cols(tp * n_kv + g, HEAD_SIZE)], sem_dkv_l.at[a, g])

    def dkv_remote(a, g):
        return pltpu.make_async_remote_copy(
            dkv_stage.at[g, a, theirs], dkvs[a].at[:, cols(tp * n_kv + g, HEAD_SIZE)],
            sem_dkv_s.at[a, g], sem_dkv_r.at[a, g], device_id=(ctx, other), device_id_type=MESH)

    def start_remote(g):
        for a in (0, 1):
            narrow_remote(a, g).start()

    def forward_first(a, g):
        narrow_local(a, g).wait()
        narrow_remote(a, g).wait_recv()
        kv_y(a, g, 0).start()

    for a in (0, 1):
        narrow_local(a, 0).start()
    wide_local(0, 0).start()

    pl.semaphore_wait(barrier, 6)
    start_remote(0)
    wide_remote(0, 0).start()
    start_remote(1)
    forward_first(0, 0)
    for d in (1, 3, 2):

        @pl.when(x + d < ROW)
        def _(d=d):
            kv_x(0, 0, d).start()

    forward_first(1, 0)
    for g in range(1, n_kv):
        for a in (0, 1):
            narrow_local(a, g).start()
        if g > 1:
            start_remote(g)
    for g in range(1, n_kv - 1):
        for a in (0, 1):
            forward_first(a, g)

    for g in range(n_kv):
        for a in (0, 1, 2):
            if (a, g) != (0, 0):
                wide_remote(a, g).start()
                wide_local(a, g).start()

    first = (ctx * SHARD).astype(F32)
    docs = len_ref.shape[1]
    lens = len_ref[...].astype(F32)
    r_d = lax.broadcasted_iota(jnp.int32, (docs, docs), 0)
    c_d = lax.broadcasted_iota(jnp.int32, (docs, docs), 1)
    starts = jnp.sum(jnp.where(c_d < r_d, jnp.broadcast_to(lens, (docs, docs)), 0.0), axis=1, keepdims=True)
    pos = lax.broadcasted_iota(jnp.int32, (docs, SHARD), 1).astype(F32) + first
    begin = jnp.max(jnp.where(starts <= pos, jnp.broadcast_to(starts, (docs, SHARD)), 0.0), axis=0, keepdims=True)
    begin = jnp.broadcast_to(begin, (SHARD, SHARD)).T
    q_row = lax.broadcasted_iota(jnp.int32, (SHARD, SHARD), 0).astype(F32) + first
    k_row = lax.broadcasted_iota(jnp.int32, (SHARD, SHARD), 1).astype(F32) + first

    def write_bias(s, carry):
        k_pos = k_row - (s * SHARD).astype(F32)
        keep = (k_pos >= begin) & (k_pos <= q_row)
        bias[s] = jnp.where(keep, 0.0, NEG)
        return carry

    lax.fori_loop(0, SLOTS, write_bias, 0)

    def forward_x(a, g):
        kv_y(a, g, 0).wait_recv()
        for d in (1, 3, 2):
            kv_x(a, g, d).start()

    def forward_y(a, g, d):
        kv_x(a, g, d).wait_recv()
        kv_y(a, g, d).start()

    def back_x(g, d):
        par = lax.rem(g, 2)
        for a in (0, 1):
            ret_y(a, g, ROW + d).wait_recv()
            ret_out[g, d - 1, a] = (acc[par, d, a] + ret_in[g, ROW + d - 1, a].astype(F32)).astype(BF16)
            ret_x(a, g, d).start()

    def back_y(g):
        par = lax.rem(g, 2)
        for a in (0, 1):
            far = acc[par, ROW, a]
            near = acc[par, 0, a]
            for d in (1, 2, 3):
                ret_x(a, g, d).wait_recv()
                part = ret_in[g, d - 1, a].astype(F32)
                crosses = ((x + d) // ROW).astype(F32)
                far = far + part * crosses
                near = near + part * (1.0 - crosses)
            ret_out[g, ROW - 1, a] = far.astype(BF16)
            ret_y(a, g, ROW).start()
            acc[par, 0, a] = near

    def back_end(g):
        par = lax.rem(g, 2)
        for a in (0, 1):
            ret_y(a, g, ROW).wait_recv()
            total = acc[par, 0, a] + ret_in[g, ROW - 1, a].astype(F32)
            dkv_stage[g, a] = total.T.astype(BF16)
            dkv_remote(a, g).start()
            dkv_local(a, g).start()

    def lanes(h, size):
        return pl.ds(pl.multiple_of(h * size, size), size)

    def head_cols(h):
        return slice(h * HEAD_SIZE, (h + 1) * HEAD_SIZE)

    def head_rows(h):
        return slice(h * SHARD, (h + 1) * SHARD)

    def twice(t):
        return jnp.concatenate([t, t], axis=1)

    sbufs = (sbuf0, sbuf1)
    topss = (tops0, tops1)

    def halves_max(sc):
        return jnp.maximum(sc[:, :HEAD_SIZE], sc[:, HEAD_SIZE:])

    def scores_step(g, s):
        keys_t = kv[0, g, s].T
        for h in range(width):
            tops = topss[h % 2]
            sc = dot_nn(qgo[0, g, :, head_cols(h)], keys_t)
            sc = sc * to_exp2 + bias[s]
            sbufs[h % 2][s, h // 2] = sc
            tops[h // 2] = jnp.maximum(tops[h // 2], halves_max(sc))

    def dq_head(g, h):
        par = lax.rem(g, 2)
        left = jnp.concatenate([dsc[par, s, lanes(h, SHARD)] for s in range(SLOTS)], axis=1)
        right = kv[0, g].reshape(SLOTS * SHARD, HEAD_SIZE)
        dq_stage[par, :, lanes(h, HEAD_SIZE)] = (dot_nn(left, right) * inv_root).astype(BF16)

    def exponentials(sbuf, hb, top, slots):
        total = jnp.zeros((SHARD, HEAD_SIZE), F32)
        for s in slots:
            e = jnp.exp2(sbuf[s, hb] - top)
            sbuf[s, hb] = e
            total = total + (e[:, :HEAD_SIZE] + e[:, HEAD_SIZE:])
        return total

    def turn_and_delta(g, h):
        q_h = qgo[0, g, :, lanes(h, HEAD_SIZE)]
        g_h = qgo[1, g, :, lanes(h, HEAD_SIZE)]
        o_h = qgo[2, g, :, lanes(h, HEAD_SIZE)]
        q_t[:, lanes(h, SHARD)] = q_h.T
        g_t[:, lanes(h, SHARD)] = g_h.T
        delta = jnp.sum(g_h.astype(F32) * o_h.astype(F32), axis=1, keepdims=True)
        deltas[h] = jnp.broadcast_to(delta, (SHARD, HEAD_SIZE))

    def near_softmax(j, carry):
        for par in (0, 1):
            h = 2 * j + par
            top = jnp.max(topss[par][j], axis=1, keepdims=True)
            invs[0, h] = jnp.broadcast_to(top, (SHARD, HEAD_SIZE))
            deltas[h] = exponentials(sbufs[par], j, top, range(ROW + 1))
        return carry

    def far_softmax(j, carry):
        for par in (0, 1):
            h = 2 * j + par
            top = jnp.max(topss[par][j], axis=1, keepdims=True)
            shrink = jnp.exp2(invs[0, h] - top)
            total = deltas[h] * shrink + exponentials(sbufs[par], j, top, range(ROW + 1, SLOTS))
            inv = jnp.broadcast_to(1.0 / jnp.sum(total, axis=1, keepdims=True), (SHARD, HEAD_SIZE))
            invs[1, h] = inv
            invs[0, h] = inv * shrink
            turn_and_delta(0, h)
        return carry

    def heads_step(g, new, old, before):
        if new is not None:
            h = 2 * new[0] + new[1]
            h_new = h
            q_new = qgo[0, g, :, lanes(h, HEAD_SIZE)]
            reach = None
        if old is not None:
            h = 2 * old[0] + old[1]
            sbuf = sbufs[old[1]]
            top = jnp.max(topss[old[1]][old[0]], axis=1, keepdims=True)
            total = jnp.zeros((SHARD, HEAD_SIZE), F32)
        for s in range(SLOTS):
            if old is not None:
                e = jnp.exp2(sbuf[s, old[0]] - top)
                sbuf[s, old[0]] = e
                total = total + (e[:, :HEAD_SIZE] + e[:, HEAD_SIZE:])
            if new is not None:
                sc = dot_nn(q_new, k_t[s]) * to_exp2 + bias[s]
                sbufs[new[1]][s, new[0]] = sc
                reach = halves_max(sc) if reach is None else jnp.maximum(reach, halves_max(sc))
                if s == SLOTS - 1 and before is not None:
                    dq_head(before, h_new)
        if new is not None:
            topss[new[1]][new[0]] = reach
        if old is not None:
            turn_and_delta(g, h)
            inv = jnp.broadcast_to(1.0 / jnp.sum(total, axis=1, keepdims=True), (SHARD, HEAD_SIZE))
            invs[1, h] = inv
            invs[0, h] = inv

    def grads_step(g, s):
        values_t = kv[1, g, s].T
        par = lax.rem(g, 2)
        far = lax.select(s > ROW, 1, 0)
        for h in range(width):
            g_h = qgo[1, g, :, head_cols(h)]
            p = sbufs[h % 2][s, h // 2] * twice(invs[far, h])
            dp = dot_nn(g_h, values_t)
            probs[head_rows(h)] = p.astype(BF16)
            dsc[par, s, head_rows(h)] = (p * (dp - twice(deltas[h]))).astype(BF16)
        dk = dot_nn(q_t[...], dsc[par, s]) * inv_root
        dv = dot_nn(g_t[...], probs[...])
        return dk, dv

    def send_dq(g):
        dq_remote(g).start()
        dq_local(g).start()

    def head_step(g, carry):
        par = lax.rem(g, 2)
        wide_local(0, g).wait()
        wide_remote(0, g).wait_recv()

        @pl.when(g > 1)
        def _():
            back_y(g - 2)

        @pl.when(g == 0)
        def _():
            tops0[...] = jnp.full(tops0.shape, 2 * NEG, F32)
            tops1[...] = jnp.full(tops1.shape, 2 * NEG, F32)

            def scores_of(i, carry_a):
                d = lax.select(i < 5, lax.select(i == 3, 3, lax.select(i == 4, 2, 1)),
                               lax.select(i == 6, 3, lax.select(i == 7, 2, 1)))
                s = lax.select(i == 0, 0, lax.select(i == 1, ROW, lax.select(i < 5, d, ROW + d)))

                @pl.when(i == 1)
                def _():
                    kv_y(0, g, 0).wait_recv()
                    for e in (1, 3, 2):

                        @pl.when(x + e >= ROW)
                        def _(e=e):
                            kv_x(0, g, e).start()

                @pl.when(i == 2)
                def _():
                    forward_x(1, g)

                @pl.when((i >= 2) & (i < 5))
                def _():
                    forward_y(0, g, d)

                @pl.when(i == 5)
                def _():
                    for a in (0, 1):
                        forward_x(a, 1)
                    lax.fori_loop(0, width // 2, near_softmax, 0)
                    for e in (1, 3, 2):
                        forward_y(1, g, e)
                    for a in (0, 1):
                        forward_first(a, n_kv - 1)

                @pl.when(i >= 5)
                def _():
                    kv_y(0, g, d).wait_recv()

                scores_step(g, s)
                return carry_a

            lax.fori_loop(0, SLOTS, scores_of, 0)
            for a in (1, 2):
                wide_local(a, g).wait()
                wide_remote(a, g).wait_recv()

            lax.fori_loop(0, width // 2, far_softmax, 0)

        def later_group(before):
            for d in (1, 3, 2):
                kv_y(0, g, d).wait_recv()
            for a in (1, 2):
                wide_local(a, g).wait()
                wide_remote(a, g).wait_recv()
            for s in range(SLOTS):
                k_t[s] = kv[0, g, s].T
            heads_step(g, (0, 0), None, before)

            def heads_of(j, carry_s):
                heads_step(g, (j, 1), (j, 0), before)
                heads_step(g, (j + 1, 0), (j, 1), before)
                return carry_s

            lax.fori_loop(0, width // 2 - 1, heads_of, 0)
            tail = width // 2 - 1
            heads_step(g, (tail, 1), (tail, 0), before)
            heads_step(g, None, (tail, 1), None)

        @pl.when((g > 0) & (g < n_kv - 1))
        def _():
            later_group(g - 1)
            send_dq(g - 1)

        @pl.when(g == n_kv - 1)
        def _():
            later_group(None)

        def grads_of(i, carry_b):
            s = lax.select(i < 3, i + 5, lax.rem(i + 3, 5))

            @pl.when((g < n_kv - 1) & (i == 0))
            def _():
                for a in (0, 1):
                    for d in (1, 3, 2):
                        forward_y(a, g + 1, d)

            @pl.when((g < n_kv - 2) & (i == 4))
            def _():
                for a in (0, 1):
                    forward_x(a, g + 2)

            @pl.when((g > 0) & (i == 0))
            def _():
                for d in (1, 2, 3):
                    back_x(g - 1, d)

            @pl.when((g > 1) & (i == 0))
            def _():
                back_end(g - 2)

            @pl.when(i < 3)
            def _():
                kv_y(1, g, i + 1).wait_recv()

            dk, dv = grads_step(g, s)

            @pl.when(i < 3)
            def _():
                ret_out[g, s - 1, 0] = dk.astype(BF16)
                ret_y(0, g, s).start()
                ret_out[g, s - 1, 1] = dv.astype(BF16)
                ret_y(1, g, s).start()

            @pl.when(i >= 3)
            def _():
                acc[par, s, 0] = dk
                acc[par, s, 1] = dv

            return carry_b

        lax.fori_loop(0, SLOTS, grads_of, 0)
        return carry

    lax.fori_loop(0, n_kv, head_step, 0)
    last = jnp.int32(n_kv - 1)

    def last_dq(i, carry):
        dq_head(last - 1 + i // width, lax.rem(i, width))
        return carry

    def drain_early(g, carry):
        for a in (0, 1, 2):
            wide_remote(a, g).wait_send()
        for a in (0, 1):
            narrow_remote(a, g).wait_send()
            for d in range(ROW):
                kv_y(a, g, d).wait_send()
            for d in (1, 2, 3):
                kv_x(a, g, d).wait_send()
        return carry

    back_x(last, 1)
    def drain(g, carry):
        for a in (0, 1):
            for s in range(ROW, SLOTS):
                ret_y(a, g, s).wait_send()
            for d in (1, 2, 3):
                ret_x(a, g, d).wait_send()
            dkv_local(a, g).wait()
            dkv_remote(a, g).wait()
        return carry

    for g in range(n_kv - 2):
        dq_local(g).wait()
        dq_remote(g).wait_send()
    half = width // 2
    lax.fori_loop(0, half, last_dq, 0)
    back_y(last - 1)
    back_x(last, 2)
    lax.fori_loop(half, 3 * half, last_dq, 0)
    back_x(last, 3)
    send_dq(last - 1)
    lax.fori_loop(3 * half, 4 * half, last_dq, 0)
    send_dq(last)
    back_end(last - 1)
    lax.fori_loop(0, n_kv, drain_early, 0)
    back_y(last)
    lax.fori_loop(0, n_kv - 1, drain, 0)
    back_end(last)

    drain(last, 0)
    for g in range(n_kv):
        if g >= n_kv - 2:
            dq_local(g).wait()
            dq_remote(g).wait_send()
        dq_remote(g).wait_recv()


def per_device(queries, key_matrix, value_matrix, attention_output, output_gradient, lengths):
    n_ctx = lax.axis_size("ctx")
    n_tp = lax.axis_size("tp")
    heads_q = queries.shape[1] // HEAD_SIZE
    heads_kv = key_matrix.shape[1] // HEAD_SIZE
    n_kv = heads_kv // n_tp
    width = heads_q // heads_kv
    wide = width * HEAD_SIZE
    dma = pltpu.SemaphoreType.DMA
    flops = 5 * 2 * SHARD * SLOTS * SHARD * HEAD_SIZE * n_kv * width
    raw = pl.pallas_call(
        functools.partial(kernel, n_ctx, n_kv, width),
        out_shape=(
            jax.ShapeDtypeStruct(queries.shape, BF16),
            jax.ShapeDtypeStruct(key_matrix.shape, BF16),
            jax.ShapeDtypeStruct(value_matrix.shape, BF16),
        ),
        in_specs=[pl.BlockSpec(memory_space=pl.ANY)] * 5 + [pl.BlockSpec(memory_space=pltpu.VMEM)],
        out_specs=(pl.BlockSpec(memory_space=pl.ANY),) * 3,
        scratch_shapes=[
            pltpu.VMEM((3, n_kv, SHARD, wide), BF16),
            pltpu.VMEM((2, n_kv, SLOTS, SHARD, HEAD_SIZE), BF16),
            pltpu.VMEM((SLOTS, width // 2, SHARD, SHARD), F32),
            pltpu.VMEM((SLOTS, width // 2, SHARD, SHARD), F32),
            pltpu.VMEM((SLOTS, SHARD, SHARD), F32),
            pltpu.VMEM((width // 2, SHARD, HEAD_SIZE), F32),
            pltpu.VMEM((width // 2, SHARD, HEAD_SIZE), F32),
            pltpu.VMEM((SLOTS, HEAD_SIZE, SHARD), BF16),
            pltpu.VMEM((2, width, SHARD, HEAD_SIZE), F32),
            pltpu.VMEM((width, SHARD, HEAD_SIZE), F32),
            pltpu.VMEM((HEAD_SIZE, width * SHARD), BF16),
            pltpu.VMEM((HEAD_SIZE, width * SHARD), BF16),
            pltpu.VMEM((width * SHARD, SHARD), BF16),
            pltpu.VMEM((2, SLOTS, width * SHARD, SHARD), BF16),
            pltpu.VMEM((2, ROW + 1, 2, HEAD_SIZE, SHARD), F32),
            pltpu.VMEM((n_kv, SLOTS - 1, 2, HEAD_SIZE, SHARD), BF16),
            pltpu.VMEM((n_kv, SLOTS - 1, 2, HEAD_SIZE, SHARD), BF16),
            pltpu.VMEM((2, SHARD, wide), BF16),
            pltpu.VMEM((n_kv, 2, SHARD, HEAD_SIZE), BF16),
            dma((3, n_kv)),
            dma((3, n_kv)),
            dma((3, n_kv)),
            dma((2, n_kv)),
            dma((2, n_kv)),
            dma((2, n_kv)),
            dma((2, n_kv, SLOTS)),
            dma((2, n_kv, SLOTS)),
            dma((2, n_kv, SLOTS)),
            dma((2, n_kv, SLOTS)),
            dma((n_kv,)),
            dma((n_kv,)),
            dma((n_kv,)),
            dma((2, n_kv)),
            dma((2, n_kv)),
            dma((2, n_kv)),
        ],
        compiler_params=pltpu.CompilerParams(
            collective_id=0, has_side_effects=True, vmem_limit_bytes=64 * 1024 * 1024 - 65536
        ),
        cost_estimate=pl.CostEstimate(
            flops=flops, bytes_accessed=10 * 1024 * 1024, transcendentals=flops // (10 * HEAD_SIZE)
        ),
        name="attention_backward",
    )(
        queries,
        key_matrix,
        value_matrix,
        attention_output,
        output_gradient,
        lengths.reshape(1, lengths.shape[0]),
    )
    return hand_over(*raw)


def hand_over_kernel(parts, dq_in, dk_in, dv_in, dq_out, dk_out, dv_out, dq_mid, dk_mid, dv_mid, sem_in, sem_out):
    rows = HALF // parts
    pieces = [(dk_in, dk_mid, dk_out), (dv_in, dv_mid, dv_out)]
    for i in range(parts):
        part = pl.ds(i * rows, rows)
        pieces.append((dq_in.at[part], dq_mid.at[part], dq_out.at[part]))
    loads = [pltpu.make_async_copy(a, b, sem_in.at[i]) for i, (a, b, _) in enumerate(pieces)]
    stores = [pltpu.make_async_copy(b, c, sem_out.at[i]) for i, (_, b, c) in enumerate(pieces)]
    for load in loads:
        load.start()
    for load, store in zip(loads, stores):
        load.wait()
        store.start()
    for store in stores:
        store.wait()


def hand_over(dq, dk, dv):
    parts = 8
    any_spec = pl.BlockSpec(memory_space=pl.ANY)
    arrays = (dq, dk, dv)
    return pl.pallas_call(
        functools.partial(hand_over_kernel, parts),
        out_shape=tuple(jax.ShapeDtypeStruct(t.shape, t.dtype) for t in arrays),
        in_specs=[any_spec] * 3,
        out_specs=(any_spec,) * 3,
        scratch_shapes=[pltpu.VMEM(t.shape, t.dtype) for t in arrays]
        + [pltpu.SemaphoreType.DMA((parts + 2,)), pltpu.SemaphoreType.DMA((parts + 2,))],
        name="hand_over",
    )(*arrays)


def solution(mesh):
    rows = P(("ctx", "tp"), None)
    return jax.shard_map(
        per_device,
        mesh=mesh,
        in_specs=(rows, rows, rows, rows, rows, P()),
        out_specs=(rows, rows, rows),
        check_vma=False,
    )
```
